128 devices in a mesh: gx: 32 (over z, x, core), gy: 4 (over y).
Axes of the slice: x: 4, y: 4, z: 4, core: 2. Of those that a mesh axis runs over, the one named last changes fastest.
Arguments:
- misfit: float32 [131072, 2, 256], P(('gx', 'gy')), may hold values from -6 to 6
- owners: int32 [131072], P(('gx', 'gy')), may hold values from 0 to 127, as said below
- offsets: int32 [131072], P(('gx', 'gy')), may hold values from 0 to 130816, as said below
- counts: int32 [128], P(('gx', 'gy')), may hold values from 640 to 1024
- viscosity: float32 [1024, 16384], P('gy', 'gx'), may hold values from 0.05 to 0.5
- friction: float32 [1024, 16384], P('gy', 'gx'), may hold values from 0.2 to 2
Outputs:
- adjoint_field: float32 [2, 1024, 16384], P(None, 'gy', 'gx')
- residual: float32 [2, 1024, 16384], P(None, 'gy', 'gx')
The draws below stay inside these ranges and needn't reach their ends.
Inputs may be any that keep to these rules, and one draw needn't show every extreme that they name: `owners`: within the slots of one device no owner is named more than 8 times; the first 8 slots of every device name one common owner, drawn from the seed. `offsets`: A segment's 256 pixels stay in one row of its owner's block.
All inputs are finite; a program needn't handle non-finite values.
Results may differ from the reference program's by a relative error of at most 0.00021.
Values sent between devices are 32-bit elements; how exact they have to be, the bound alone decides.
A program may use at most 64 MiB of HBM per device.

```python
import math
import jax
import jax.numpy as jnp

CX = 512
CY = 256
PIX = 256
PAIR_CAP = 8
ITERS = 3
SEG_DEV = 1024
SEGS = 131072
NX = 16384
NY = 1024
N_GX = 32
N_GY = 4


def draw_owners(key, part):
    key = jax.random.fold_in(key, 11)
    ndev = N_GX * N_GY
    common = jax.random.randint(jax.random.fold_in(key, 0), (), 0, ndev)
    base = (jnp.arange(ndev * PAIR_CAP, dtype=jnp.int32) // PAIR_CAP + common) % ndev
    keys = jax.random.split(jax.random.fold_in(key, 1), ndev)

    def one_device(device_key):
        tail = jax.random.permutation(device_key, base[PAIR_CAP:])
        return jnp.concatenate([base[:PAIR_CAP], tail])[:SEG_DEV]
    return jax.vmap(one_device)(keys).reshape(-1).astype(jnp.int32)


def draw_offsets(key, part):
    key = jax.random.fold_in(key, 23)
    rows = jax.random.randint(jax.random.fold_in(key, 0), (SEGS,), 0, CY)
    columns = jax.random.randint(jax.random.fold_in(key, 1), (SEGS,), 0, CX - PIX + 1)
    result = (rows * CX + columns).astype(jnp.int32)
    result = result.at[0].set((CY - 1) * CX + CX - PIX)
    result = result.at[1].set(0)
    return result


def draw_counts(key, part):
    key = jax.random.fold_in(key, 37)
    ndev = N_GX * N_GY
    lowest = max(5 * SEG_DEV // 8, PAIR_CAP)
    result = jax.random.randint(jax.random.fold_in(key, 0), (ndev,), lowest, SEG_DEV + 1)
    first = jax.random.randint(jax.random.fold_in(key, 1), (), 0, ndev)
    second = (first + 1 + jax.random.randint(jax.random.fold_in(key, 2), (), 0, ndev - 1)) % ndev
    result = result.at[first].set(SEG_DEV)
    result = result.at[second].set(lowest)
    return result.astype(jnp.int32)


def steps_of(own_key, dims, shards, low, high):
    gain, own = 1.0, jax.random.fold_in(own_key, 6)
    for position, blocks in shards:
        draws = jnp.exp(jax.random.uniform(jax.random.fold_in(own, position), (blocks,), jnp.float32, low / len(shards), high / len(shards)))
        gain = gain * jnp.repeat(draws, dims[position] // blocks).reshape([-1 if axis == position else 1 for axis in range(len(dims))])
    return gain


def noise(stream_key, shape, width, reach, cuts=(), kind=jnp.bfloat16):
    drawn = jax.random.normal(stream_key, shape, jnp.float32) * width
    if len(cuts) > 0:
        drawn = steps_of(stream_key, shape, cuts, -0.22, 0.18) * drawn
    return jnp.clip(drawn, min=-reach, max=reach).astype(kind)


def setup_inputs(seed: int = 0) -> dict:
    streams_of = jax.random.split(jax.random.key(seed), 7)
    return {
        "misfit": noise(streams_of[0], (SEGS, 2, PIX), 1.0, 6.0, ((0, 128),), jnp.float32),
        "owners": draw_owners(jax.random.fold_in(streams_of[6], 71), 0),
        "offsets": draw_offsets(jax.random.fold_in(streams_of[6], 71), 0),
        "counts": draw_counts(jax.random.fold_in(streams_of[6], 71), 0),
        "viscosity": jnp.clip(jnp.exp(math.log(0.5) - 2.3025851 * jax.random.uniform(streams_of[4], (NY, NX), jnp.float32) ** steps_of(streams_of[4], (NY, NX), ((0, 4), (1, 32)), -0.2, 0.2)), 0.05, 0.5),
        "friction": jnp.clip(jnp.exp(math.log(2.0) - 2.3025851 * jax.random.uniform(streams_of[5], (NY, NX), jnp.float32) ** steps_of(streams_of[5], (NY, NX), ((0, 4), (1, 32)), -0.2, 0.2)), 0.2, 2.0),
    }


def node_viscosity(padded_eta):
    return 0.25 * (padded_eta[:-1, :-1] + padded_eta[1:, :-1] + padded_eta[:-1, 1:] + padded_eta[1:, 1:])


def shelf_operator(padded, node_eta, friction, field):
    pu = padded[0]
    pv = padded[1]
    exx = pu[:-1, 1:] - pu[:-1, :-1]
    eyy = pv[1:, :-1] - pv[:-1, :-1]
    exy = 0.5 * (pu[1:, :-1] - pu[:-1, :-1] + pv[:-1, 1:] - pv[:-1, :-1])
    sxx = node_eta * (4.0 * exx + 2.0 * eyy)
    syy = node_eta * (2.0 * exx + 4.0 * eyy)
    sxy = 4.0 * node_eta * exy
    image_u = sxx[1:, :-1] - sxx[1:, 1:] + 0.5 * (sxy[:-1, 1:] - sxy[1:, 1:]) + friction * field[0]
    image_v = syy[:-1, 1:] - syy[1:, 1:] + 0.5 * (sxy[1:, :-1] - sxy[1:, 1:]) + friction * field[1]
    return jnp.stack([image_u, image_v])


def reference(misfit, owners, offsets, counts, viscosity, friction):
    ndev = N_GX * N_GY
    slot = jnp.arange(SEG_DEV, dtype=jnp.int32)
    live = (slot[None, :] < counts[:, None]).reshape(-1)
    owner_x = owners // N_GY
    owner_y = owners % N_GY
    row = owner_y * CY + offsets // CX
    column = owner_x * CX + offsets % CX
    flat = (row * NX + column).astype(jnp.int32)
    index = flat[:, None] + jnp.arange(PIX, dtype=jnp.int32)[None, :]
    values = misfit * live[:, None, None].astype(jnp.float32)
    rhs = jnp.zeros((2, NY * NX), jnp.float32)
    rhs = rhs.at[:, index].add(jnp.moveaxis(values, 1, 0))
    rhs = rhs.reshape(2, NY, NX)
    node_eta = node_viscosity(jnp.pad(viscosity, 1))

    def apply(field):
        padded = jnp.pad(field, ((0, 0), (1, 1), (1, 1)))
        return shelf_operator(padded, node_eta, friction, field)

    adjoint_field = jnp.zeros_like(rhs)
    residual = rhs
    direction = rhs
    norm_now = jnp.sum(residual * residual)
    for step in range(ITERS):
        image = apply(direction)
        alpha = norm_now / jnp.sum(direction * image)
        adjoint_field = adjoint_field + alpha * direction
        residual = residual - alpha * image
        norm_next = jnp.sum(residual * residual)
        direction = residual + (norm_next / norm_now) * direction
        norm_now = norm_next
    return adjoint_field, residual
```

```python
import functools

import jax
import jax.numpy as jnp
from jax import lax
from jax.experimental import pallas as pl
from jax.experimental.pallas import tpu as pltpu
from jax.sharding import PartitionSpec as P

MESH = pl.DeviceIdType.MESH
CAP = 8
LANES = 128
HALO = 8
MSG = 33
PAD = 40
bf16, f32, i32 = jnp.bfloat16, jnp.float32, jnp.int32


def split3(x):
    hi = x.astype(bf16)
    rest = x - hi.astype(f32)
    mid = rest.astype(bf16)
    low = (rest - mid.astype(f32)).astype(bf16)
    return hi, mid, low


def iota(shape, dim):
    return lax.broadcasted_iota(i32, shape, dim)


def remote(src, dst, send_sem, recv_sem, dev):
    return pltpu.make_async_remote_copy(
        src_ref=src, dst_ref=dst, send_sem=send_sem, recv_sem=recv_sem, device_id=dev, device_id_type=MESH
    )


def kernel(
    n_gx, n_gy, chunk,
    misfit, owners, offsets, counts, viscosity, friction, out_x, out_r,
    parts, send, recv, deposit, field, nodes, q1, q2, q3, strips, halo, sums,
    a2a_send, a2a_recv, self_sem, ex_send, ex_recv, ar_send, ar_recv,
):
    ndev = n_gx * n_gy
    ix, iy = lax.axis_index("gx"), lax.axis_index("gy")
    me = ix * n_gy + iy
    slots = misfit.shape[0] // 4
    rows, columns = viscosity.shape
    chunks = ndev // chunk
    keys = chunk * CAP

    barrier = pltpu.get_barrier_semaphore()

    def greet(p, carry):
        dev = lax.rem(me + p, ndev)
        pl.semaphore_signal(barrier, inc=1, device_id=(dev // n_gy, lax.rem(dev, n_gy)), device_id_type=MESH)
        return carry

    lax.fori_loop(1, ndev, greet, 0)

    count = counts[0]
    lane_blocks = slots // LANES
    upper = (iota((LANES, LANES), 0) < iota((LANES, LANES), 1)).astype(bf16)
    carry = jnp.zeros((ndev, 1), f32)
    hots, targets, weights = [], [], []
    for b in range(lane_blocks):
        own = owners[pl.ds(b, 1), :]
        off = offsets[pl.ds(b, 1), :]
        live = (iota((1, LANES), 1) + b * LANES) < count
        rel = jnp.where(live, lax.rem(own - me + ndev, ndev), -1)
        hot = (iota((ndev, LANES), 0) == rel).astype(f32)
        before = jnp.dot(hot.astype(bf16), upper, preferred_element_type=f32) + carry
        rank = jnp.sum(hot * before, axis=0, keepdims=True).astype(i32)
        carry = carry + jnp.sum(hot, axis=1, keepdims=True)
        targets.append(jnp.where(live, rel * CAP + rank, -1))
        hots.append(hot.astype(bf16))
        mine = lax.rem(iota((LANES, LANES), 0), CAP) == rank
        row_part = jnp.where(mine, lax.shift_right_logical(off, 9).astype(f32), 0.0)
        col_part = jnp.where(mine, lax.bitwise_and(off, 511).astype(f32), 0.0)
        weights.append(jnp.concatenate([row_part, col_part], axis=0).astype(bf16))
    target = jnp.concatenate(targets, axis=1)
    hot = jnp.concatenate(hots, axis=1)
    weight = jnp.concatenate(weights, axis=1)
    meta = lax.dot_general(hot, weight, (((1,), (1,)), ((), ())), preferred_element_type=f32)
    meta = meta[:, :LANES] * 512.0 + meta[:, LANES:]
    send[:, 32, :] = meta

    for t in range(4):
        hi, mid, low = split3(misfit[pl.ds(t, slots, stride=4), :])
        parts[:, pl.ds(t * LANES, LANES)] = hi
        parts[:, pl.ds((4 + t) * LANES, LANES)] = mid
        parts[:, pl.ds((8 + t) * LANES, LANES)] = low

    pl.semaphore_wait(barrier, ndev - 1)

    def pack(g, carry):
        place = ((iota((keys, slots), 0) + g * keys) == target).astype(bf16)
        packed = jnp.dot(place, parts[...], preferred_element_type=f32)
        packed = packed[:, :512] + packed[:, 512:1024] + packed[:, 1024:]
        for t in range(4):
            send[pl.ds(g * chunk, chunk), pl.ds(t * CAP, CAP), :] = packed[:, t * LANES:(t + 1) * LANES].reshape(
                chunk, CAP, LANES
            )

        def push(i, carry):
            p = g * chunk + i
            dev = lax.rem(me + p, ndev)
            remote(
                send.at[p, pl.ds(0, MSG), :], recv.at[p, pl.ds(0, MSG), :], a2a_send.at[g], a2a_recv.at[g],
                (dev // n_gy, lax.rem(dev, n_gy)),
            ).start()
            return carry

        lax.fori_loop(jnp.where(g == 0, 1, 0), chunk, push, 0)
        return carry

    lax.fori_loop(0, chunks, pack, 0)
    own = pltpu.make_async_copy(send.at[0, pl.ds(0, MSG), :], recv.at[0, pl.ds(0, MSG), :], self_sem)
    own.start()

    left, right = lax.rem(ix + n_gx - 1, n_gx), lax.rem(ix + 1, n_gx)
    up, down = lax.rem(iy + n_gy - 1, n_gy), lax.rem(iy + 1, n_gy)
    bottom = HALO + rows
    first, last = pl.ds(0, 8), pl.ds(LANES - 8, 8)
    tile0, tile3 = pl.ds(0, LANES), pl.ds(LANES + rows, LANES)
    part0, part1, whole = pl.ds(0, LANES), pl.ds(rows - LANES, LANES), pl.ds(0, rows)
    lane_tile = iota((8, LANES), 1)
    side = jnp.where(lane_tile < 64, jnp.where(ix < n_gx - 1, 1.0, 0.0), jnp.where(ix > 0, 1.0, 0.0))
    above = jnp.where(iy > 0, 1.0, 0.0)
    below = jnp.where(iy < n_gy - 1, 1.0, 0.0)
    mask_main = jnp.concatenate([jnp.ones((8, columns), f32), side], axis=1)

    def copies(c):
        pair = pl.ds(c, 2)
        main = pl.ds(0, columns)
        moves = (
            (field.at[pair, pl.ds(HALO, 8), main], field.at[pair, pl.ds(bottom, 8), main], (ix, up)),
            (field.at[pair, pl.ds(bottom - 8, 8), main], field.at[pair, pl.ds(0, 8), main], (ix, down)),
            (strips.at[pair, first, whole], halo.at[pair, first, pl.ds(LANES, rows)], (left, iy)),
            (strips.at[pair, last, whole], halo.at[pair, last, pl.ds(LANES, rows)], (right, iy)),
            (strips.at[pair, first, part0], halo.at[pair, first, tile3], (left, up)),
            (strips.at[pair, first, part1], halo.at[pair, first, tile0], (left, down)),
            (strips.at[pair, last, part0], halo.at[pair, last, tile3], (right, up)),
            (strips.at[pair, last, part1], halo.at[pair, last, tile0], (right, down)),
        )
        h = c // 2
        return [remote(s, d, ex_send.at[h, k], ex_recv.at[h, k], dev) for k, (s, d, dev) in enumerate(moves)]

    def offer(c):
        for f in (c, c + 1):
            for j in range(rows // LANES):
                at = pl.ds(HALO + j * LANES, LANES)
                mix = jnp.where(
                    iota((LANES, LANES), 1) < 64, field[f, at, pl.ds(0, LANES)], field[f, at, pl.ds(columns - LANES, LANES)]
                )
                strips[f, :, pl.ds(j * LANES, LANES)] = mix.T
        for copy in copies(c):
            copy.start()

    def accept(c):
        for copy in copies(c):
            copy.wait_recv()
        wrap = pl.ds(columns, LANES)
        main = pl.ds(0, columns)
        for f in (c, c + 1):
            for j in range(rows // LANES):
                turned = halo[f, :, pl.ds((j + 1) * LANES, LANES)].T
                field[f, pl.ds(HALO + j * LANES, LANES), wrap] = turned * side[:1]
            field[f, pl.ds(0, 8), wrap] = halo[f, :, tile0].T[LANES - 8:] * (side * above)
            field[f, pl.ds(bottom, 8), wrap] = halo[f, :, tile3].T[:8] * (side * below)
            field[f, pl.ds(0, 8), main] = field[f, pl.ds(0, 8), main] * above
            field[f, pl.ds(bottom, 8), main] = field[f, pl.ds(bottom, 8), main] * below

    for f in range(4):
        halo[f, pl.ds(8, LANES - 16), :] = jnp.zeros((LANES - 16, halo.shape[2]), f32)
    field[0, pl.ds(HALO, rows), pl.ds(0, columns)] = viscosity[...]
    field[1, pl.ds(HALO, rows), pl.ds(0, columns)] = friction[...]
    offer(0)

    near = min(8, n_gx)
    far = ndev // near

    def stage1(s):
        low, high = lax.rem(ix, near), ix // near * near
        return [
            remote(sums.at[s, 0], sums.at[s, k], ar_send.at[s, k], ar_recv.at[s, k], (high + lax.rem(low + k, near), iy))
            for k in range(1, near)
        ]

    def stage2(s):
        low = lax.rem(ix, near)
        group = ix // near * n_gy + iy
        result = []
        for k in range(1, far):
            other = lax.rem(group + k, far)
            result.append(
                remote(
                    sums.at[s, near], sums.at[s, near + k], ar_send.at[s, near + k], ar_recv.at[s, near + k],
                    (other // n_gy * near + low, lax.rem(other, n_gy)),
                )
            )
        return result

    def add_all(s, terms):
        terms = list(terms) + [jnp.zeros((1, LANES), f32)] * (8 - len(terms))
        sums[s, 0] = jnp.concatenate(terms, axis=0)
        for copy in stage1(s):
            copy.start()
        for copy in stage1(s):
            copy.wait_recv()
        total = sums[s, 0]
        for k in range(1, near):
            total = total + sums[s, k]
        sums[s, near] = total
        for copy in stage2(s):
            copy.start()
        for copy in stage2(s):
            copy.wait_recv()
        total = sums[s, near]
        for k in range(1, far):
            total = total + sums[s, near + k]
        return jnp.sum(total, axis=1, keepdims=True)

    tiles = (rows + 2 * HALO) // 8
    width = columns + LANES

    def east(x):
        return pltpu.roll(x, width - 1, 1)

    def west(x):
        return pltpu.roll(x, 1, 1)

    sub = iota((8, width), 0)

    def south(x, following):
        return pltpu.roll(jnp.where(sub == 0, following, x), 7, 0)

    def north(x, previous):
        return pltpu.roll(jnp.where(sub == 7, previous, x), 1, 0)

    def tile_at(t):
        if isinstance(t, int):
            return pl.ds(t * 8, 8)
        return pl.ds(pl.multiple_of(t * 8, 8), 8)

    accept(0)

    def node_tile(t, total):
        here = field[0, tile_at(t), :]
        following = field[0, tile_at(jnp.minimum(t + 1, tiles - 1)), :]
        pair = here + south(here, following)
        doubled = 0.5 * (pair + east(pair))
        nodes[tile_at(t), :] = doubled
        return total + 5.0 * doubled + field[1, tile_at(t), :]

    total = lax.fori_loop(0, tiles, node_tile, jnp.zeros((8, width), f32))
    total = jnp.sum(total, axis=0, keepdims=True)
    part = sum(total[:, k * LANES:(k + 1) * LANES] for k in range(columns // LANES))
    sigma = add_all(0, [part])[:1] * (1.0 / (ndev * rows * columns))

    lane16 = iota((16, LANES), 1) // CAP
    sub16 = iota((16, LANES), 0)
    own.wait()
    for g in range(chunks):
        lo = 1 if g == 0 else 0
        got = recv.at[pl.ds(g * chunk + lo, chunk - lo), pl.ds(0, MSG), :]
        pltpu.make_async_copy(got, got, a2a_recv.at[g]).wait()
        for h in range(chunk // 16):
            base = g * chunk + h * 16
            info = recv[pl.ds(base, 16), 32, :]
            off = jnp.sum(jnp.where(lane16 == sub16, info, 0.0), axis=0, keepdims=True).astype(i32)
            row_hot = (iota((rows, LANES), 0) == lax.shift_right_logical(off, 9)).astype(bf16)
            col = jnp.broadcast_to(lax.bitwise_and(off, 511).astype(f32), (LANES, LANES)).T.astype(i32)
            lane = iota((LANES, LANES), 1)
            shift = lax.bitwise_and(col, LANES - 1)
            index = lax.bitwise_and(lane - shift, LANES - 1)
            lag = lax.shift_right_logical(col, 7) + (lane < shift).astype(i32)
            spread = []
            for c in range(2):
                ab = []
                for half in range(2):
                    x = recv[pl.ds(base, 16), pl.ds((half * 2 + c) * CAP, CAP), :].reshape(LANES, LANES)
                    ab.append(jnp.take_along_axis(x, index, axis=1, mode="promise_in_bounds"))
                for t in range(4):
                    spread.append(
                        jnp.where(lag == t, ab[0], jnp.where(lag == t - 1, ab[1], 0.0))
                    )
            pieces = split3(jnp.concatenate(spread, axis=1))
            add = jnp.dot(
                jnp.concatenate([row_hot] * 3, axis=1), jnp.concatenate(pieces, axis=0), preferred_element_type=f32
            )
            if g == 0 and h == 0:
                deposit[...] = add
            elif g < chunks - 1 or h < chunk // 16 - 1:
                deposit[...] += add
            else:
                add = deposit[...] + add
                field[2, pl.ds(HALO, rows), pl.ds(0, columns)] = add[:, :columns]
                field[3, pl.ds(HALO, rows), pl.ds(0, columns)] = add[:, columns:]
    if chunks * (chunk // 16) == 1:
        field[2, pl.ds(HALO, rows), pl.ds(0, columns)] = deposit[:, :columns]
        field[3, pl.ds(HALO, rows), pl.ds(0, columns)] = deposit[:, columns:]

    offer(2)
    accept(2)

    def fold(x):
        return sum(x[:, k * LANES:(k + 1) * LANES] for k in range(columns // LANES))

    def apply(source, target, products):
        su, sv = source
        tu, tv = target

        def step(t, carry, mask, count_it):
            syy_old, sxy_old, acc = carry
            nxt = min(t + 1, tiles - 1) if isinstance(t, int) else t + 1
            here, there = tile_at(t), tile_at(nxt)
            u, v = su[here, :], sv[here, :]
            us, vs = south(u, su[there, :]), south(v, sv[there, :])
            s = nodes[here, :]
            exx = east(u) - u
            eyy = vs - v
            both = exx + eyy
            sxx = s * (exx + both)
            syy = s * (eyy + both)
            sxy = (0.5 * s) * ((us - u) + (east(v) - v))
            drag = field[1, here, :] - sigma
            au = (west(sxx) - sxx) + (north(sxy, sxy_old) - sxy) + drag * u
            av = (north(syy, syy_old) - syy) + (west(sxy) - sxy) + drag * v
            au = au * mask
            av = av * mask
            tu[here, :] = au
            tv[here, :] = av
            if count_it:
                acc = tuple(
                    a + fold(p[0] * q[0] + p[1] * q[1])
                    for a, (p, q) in zip(acc, [(((u, v), (au, av))[i], ((u, v), (au, av))[j]) for i, j in products])
                )
            return syy, sxy, acc

        zero = jnp.zeros((8, width), f32)
        carry = (zero, zero, tuple(jnp.zeros((8, LANES), f32) for _ in products))
        carry = step(0, carry, mask_main * above, False)
        carry = lax.fori_loop(1, tiles - 1, lambda t, c: step(t, c, mask_main, True), carry)
        carry = step(tiles - 1, carry, mask_main * below, False)
        return [jnp.sum(a, axis=0, keepdims=True) for a in carry[2]]

    f0 = (field.at[2], field.at[3])
    f1, f2, f3 = ((q.at[0], q.at[1]) for q in (q1, q2, q3))
    terms = apply(f0, f1, ((0, 0), (0, 1), (1, 1)))
    terms += apply(f1, f2, ((0, 1), (1, 1)))
    terms += apply(f2, f3, ((0, 1),))
    products = add_all(1, terms)

    m = [products[k:k + 1] / products[:1] for k in range(6)]

    def form(a, shifted):
        result = 0.0
        for i in range(len(a)):
            for j in range(i, len(a)):
                w = m[i + j + 1] + sigma * m[i + j] if shifted else m[i + j]
                term = a[i] * a[j] * w
                result = result + (term if i == j else 2.0 * term)
        return result

    one = jnp.ones((1, 1), f32)
    d, r, x, rr = [one], [one], [0.0 * one] * 3, one
    for k in range(3):
        alpha = rr / form(d, True)
        x = [x[i] + alpha * d[i] if i < len(d) else x[i] for i in range(3)]
        image = [sigma * d[i] for i in range(len(d))] + [0.0 * one]
        image = [image[i] + d[i - 1] if i else image[i] for i in range(len(image))]
        r = [(r[i] if i < len(r) else 0.0) - alpha * image[i] for i in range(len(image))]
        if k < 2:
            fresh = form(r, False)
            beta = fresh / rr
            d = [r[i] + (beta * d[i] if i < len(d) else 0.0) for i in range(len(r))]
            rr = fresh

    def finish(t, carry):
        here = pl.ds(pl.multiple_of(t * 8, 8), 8)
        padded = pl.ds(pl.multiple_of(t * 8 + HALO, 8), 8)
        main = pl.ds(0, columns)
        for c in range(2):
            a0, a1, a2, a3 = field[2 + c, padded, main], q1[c, padded, main], q2[c, padded, main], q3[c, padded, main]
            out_x[c, here, :] = x[0] * a0 + x[1] * a1 + x[2] * a2
            out_r[c, here, :] = r[0] * a0 + r[1] * a1 + r[2] * a2 + r[3] * a3
        return carry

    lax.fori_loop(0, rows // 8, finish, 0)

    for c in (0, 2):
        for copy in copies(c):
            copy.wait_send()
    for s in range(2):
        for copy in stage1(s) + stage2(s):
            copy.wait_send()
    for g in range(chunks):
        lo = 1 if g == 0 else 0
        sent = send.at[pl.ds(g * chunk + lo, chunk - lo), pl.ds(0, MSG), :]
        pltpu.make_async_copy(sent, sent, a2a_send.at[g]).wait()


def shards(n_gx, n_gy, misfit, owners, offsets, counts, viscosity, friction):
    ndev = n_gx * n_gy
    slots = owners.shape[0]
    rows, columns = viscosity.shape
    chunk = min(32, ndev)
    chunks = ndev // chunk
    near = min(8, n_gx)
    padded = (rows + 2 * HALO, columns + LANES)
    pixels = misfit.reshape(slots, 2, 2, LANES).transpose(0, 2, 1, 3).reshape(slots * 4, LANES)
    vmem = pl.BlockSpec(memory_space=pltpu.VMEM)
    smem = pl.BlockSpec(memory_space=pltpu.SMEM)
    out = jax.ShapeDtypeStruct((2, rows, columns), f32)
    dma = pltpu.SemaphoreType.DMA
    return pl.pallas_call(
        functools.partial(kernel, n_gx, n_gy, chunk),
        out_shape=(out, out),
        in_specs=[vmem, vmem, vmem, smem, vmem, vmem],
        out_specs=(vmem, vmem),
        scratch_shapes=[
            pltpu.VMEM((slots, 12 * LANES), bf16),
            pltpu.VMEM((ndev, PAD, LANES), f32),
            pltpu.VMEM((ndev, PAD, LANES), f32),
            pltpu.VMEM((rows, 2 * columns), f32),
            pltpu.VMEM((4,) + padded, f32),
            pltpu.VMEM(padded, f32),
            pltpu.VMEM((2,) + padded, f32),
            pltpu.VMEM((2,) + padded, f32),
            pltpu.VMEM((2,) + padded, f32),
            pltpu.VMEM((4, LANES, rows), f32),
            pltpu.VMEM((4, LANES, rows + 2 * LANES), f32),
            pltpu.VMEM((2, near + ndev // near, 8, LANES), f32),
            dma((chunks,)),
            dma((chunks,)),
            dma,
            dma((2, 8)),
            dma((2, 8)),
            dma((2, near + ndev // near)),
            dma((2, near + ndev // near)),
        ],
        compiler_params=pltpu.CompilerParams(
            collective_id=0, has_side_effects=True, vmem_limit_bytes=48 * 1024 * 1024
        ),
    )(
        pixels,
        owners.reshape(slots // LANES, LANES),
        offsets.reshape(slots // LANES, LANES),
        counts,
        viscosity,
        friction,
    )


def solution(mesh):
    in_specs = (
        P(("gx", "gy"), None, None),
        P(("gx", "gy")),
        P(("gx", "gy")),
        P(("gx", "gy")),
        P("gy", "gx"),
        P("gy", "gx"),
    )
    out_specs = (P(None, "gy", "gx"), P(None, "gy", "gx"))
    return jax.shard_map(
        functools.partial(shards, mesh.shape["gx"], mesh.shape["gy"]),
        mesh=mesh, in_specs=in_specs, out_specs=out_specs, check_vma=False,
    )
```

```python
import functools

import jax
import jax.numpy as jnp
from jax import lax
from jax.experimental import pallas as pl
from jax.experimental.pallas import tpu as pltpu
from jax.sharding import PartitionSpec as P

MESH = pl.DeviceIdType.MESH
CAP = 8
LANES = 128
HALO = 8
MSG = 33
PAD = 40
STRIDE, BACK = 37, 45
GRAIN = 1024.0
bf16, f32, i32 = jnp.bfloat16, jnp.float32, jnp.int32


def split3(x):
    hi = x.astype(bf16)
    rest = x - hi.astype(f32)
    mid = rest.astype(bf16)
    low = (rest - mid.astype(f32)).astype(bf16)
    return hi, mid, low


def iota(shape, dim):
    return lax.broadcasted_iota(i32, shape, dim)


def remote(src, dst, send_sem, recv_sem, dev):
    return pltpu.make_async_remote_copy(
        src_ref=src, dst_ref=dst, send_sem=send_sem, recv_sem=recv_sem, device_id=dev, device_id_type=MESH
    )


def kernel(
    n_gx, n_gy, chunk,
    misfit_hbm, owners_hbm, offsets_hbm, counts, viscosity_hbm, friction_hbm, out_x, out_r,
    misfit, owners, offsets, parts, send, recv, deposit, field, nodes, q1, q2, q3, strips, halo, sums,
    in_sem, a2a_send, a2a_recv, self_sem, ex_send, ex_recv, ar_send, ar_recv,
):
    ndev = n_gx * n_gy
    ix, iy = lax.axis_index("gx"), lax.axis_index("gy")
    me = ix * n_gy + iy
    slots = misfit.shape[0] // 4
    rows, columns = viscosity_hbm.shape
    chunks = ndev // chunk
    keys = chunk * CAP
    gx_dims = (4, 4, 2) if n_gx == 32 else (n_gx // 2, 2)

    def ahead(p):
        dev = lax.rem(me + p * STRIDE, ndev)
        return dev // n_gy, lax.rem(dev, n_gy)

    barrier = pltpu.get_barrier_semaphore()

    def greet(p, carry):
        pl.semaphore_signal(barrier, inc=1, device_id=ahead(p), device_id_type=MESH)
        return carry

    loads = [
        pltpu.make_async_copy(src, dst, in_sem.at[k])
        for k, (src, dst) in enumerate(
            (
                (owners_hbm, owners),
                (offsets_hbm, offsets),
                (viscosity_hbm, field.at[0, pl.ds(HALO, rows), pl.ds(0, columns)]),
                (friction_hbm, field.at[1, pl.ds(HALO, rows), pl.ds(0, columns)]),
                (misfit_hbm, misfit),
            )
        )
    ]
    for load in loads:
        load.start()
    lax.fori_loop(1, ndev, greet, 0)
    loads[0].wait()
    loads[1].wait()

    count = counts[0]
    lane_blocks = slots // LANES
    upper = (iota((LANES, LANES), 0) < iota((LANES, LANES), 1)).astype(bf16)
    carry = jnp.zeros((ndev, 1), f32)
    hots, targets, weights = [], [], []
    for b in range(lane_blocks):
        own = owners[pl.ds(b, 1), :]
        off = offsets[pl.ds(b, 1), :]
        live = (iota((1, LANES), 1) + b * LANES) < count
        rel = jnp.where(live, lax.rem((own - me + ndev) * BACK, ndev), -1)
        hot = (iota((ndev, LANES), 0) == rel).astype(f32)
        before = jnp.dot(hot.astype(bf16), upper, preferred_element_type=f32) + carry
        rank = jnp.sum(hot * before, axis=0, keepdims=True).astype(i32)
        carry = carry + jnp.sum(hot, axis=1, keepdims=True)
        targets.append(jnp.where(live, rel * CAP + rank, -1))
        hots.append(hot.astype(bf16))
        mine = lax.rem(iota((LANES, LANES), 0), CAP) == rank
        row_part = jnp.where(mine, lax.shift_right_logical(off, 9).astype(f32), 0.0)
        col_part = jnp.where(mine, lax.bitwise_and(off, 511).astype(f32), 0.0)
        weights.append(jnp.concatenate([row_part, col_part], axis=0).astype(bf16))
    target = jnp.concatenate(targets, axis=1)
    hot = jnp.concatenate(hots, axis=1)
    weight = jnp.concatenate(weights, axis=1)
    meta = lax.dot_general(hot, weight, (((1,), (1,)), ((), ())), preferred_element_type=f32)
    meta = meta[:, :LANES] * 512.0 + meta[:, LANES:]

    loads[2].wait()
    loads[3].wait()

    def share_tile(t, total):
        here = pl.ds(pl.multiple_of(t * 8 + HALO, 8), 8)
        return total + 10.0 * field[0, here, pl.ds(0, columns)] + field[1, here, pl.ds(0, columns)]

    share = lax.fori_loop(0, rows // 8, share_tile, jnp.zeros((8, columns), f32), unroll=4)
    share = jnp.sum(jnp.sum(share, axis=0, keepdims=True), axis=1, keepdims=True)
    share = jnp.round(share * (GRAIN / (rows * columns)))
    send[:, 32, :] = jnp.where(iota((ndev, LANES), 1) < 64, meta, share)

    loads[4].wait()
    for t in range(4):
        hi, mid, low = split3(misfit[pl.ds(t, slots, stride=4), :])
        parts[:, pl.ds(t * LANES, LANES)] = hi
        parts[:, pl.ds((4 + t) * LANES, LANES)] = mid
        parts[:, pl.ds((8 + t) * LANES, LANES)] = low

    def pack(g):
        place = ((iota((keys, slots), 0) + g * keys) == target).astype(bf16)
        packed = jnp.dot(place, parts[...], preferred_element_type=f32)
        packed = packed[:, :512] + packed[:, 512:1024] + packed[:, 1024:]
        for t in range(4):
            send[pl.ds(g * chunk, chunk), pl.ds(t * CAP, CAP), :] = packed[:, t * LANES:(t + 1) * LANES].reshape(
                chunk, CAP, LANES
            )

    def push(g):
        def one(p, carry):
            remote(
                send.at[p, pl.ds(0, MSG), :], recv.at[p, pl.ds(0, MSG), :], a2a_send.at[g], a2a_recv.at[g], ahead(p)
            ).start()
            return carry

        lax.fori_loop(max(g * chunk, 1), (g + 1) * chunk, one, 0)

    left, right = lax.rem(ix + n_gx - 1, n_gx), lax.rem(ix + 1, n_gx)
    up, down = lax.rem(iy + n_gy - 1, n_gy), lax.rem(iy + 1, n_gy)
    bottom = HALO + rows
    first, last = pl.ds(0, 8), pl.ds(LANES - 8, 8)
    tile0, tile3 = pl.ds(0, LANES), pl.ds(LANES + rows, LANES)
    part0, part1, whole = pl.ds(0, LANES), pl.ds(rows - LANES, LANES), pl.ds(0, rows)
    lane_tile = iota((8, LANES), 1)
    side = jnp.where(lane_tile < 64, jnp.where(ix < n_gx - 1, 1.0, 0.0), jnp.where(ix > 0, 1.0, 0.0))
    above = jnp.where(iy > 0, 1.0, 0.0)
    below = jnp.where(iy < n_gy - 1, 1.0, 0.0)
    mask_main = jnp.concatenate([jnp.ones((8, columns), f32), side], axis=1)

    def copies(c):
        pair = pl.ds(c, 2)
        main = pl.ds(0, columns)
        moves = (
            (field.at[pair, pl.ds(HALO, 8), main], field.at[pair, pl.ds(bottom, 8), main], (ix, up)),
            (field.at[pair, pl.ds(bottom - 8, 8), main], field.at[pair, pl.ds(0, 8), main], (ix, down)),
            (strips.at[pair, first, whole], halo.at[pair, first, pl.ds(LANES, rows)], (left, iy)),
            (strips.at[pair, last, whole], halo.at[pair, last, pl.ds(LANES, rows)], (right, iy)),
            (strips.at[pair, first, part0], halo.at[pair, first, tile3], (left, up)),
            (strips.at[pair, first, part1], halo.at[pair, first, tile0], (left, down)),
            (strips.at[pair, last, part0], halo.at[pair, last, tile3], (right, up)),
            (strips.at[pair, last, part1], halo.at[pair, last, tile0], (right, down)),
        )
        h = c // 2
        return [remote(s, d, ex_send.at[h, k], ex_recv.at[h, k], dev) for k, (s, d, dev) in enumerate(moves)]

    def offer(c):
        for f in (c, c + 1):
            for j in range(rows // LANES):
                at = pl.ds(HALO + j * LANES, LANES)
                mix = jnp.where(
                    iota((LANES, LANES), 1) < 64, field[f, at, pl.ds(0, LANES)], field[f, at, pl.ds(columns - LANES, LANES)]
                )
                strips[f, :, pl.ds(j * LANES, LANES)] = mix.T

    def accept(c):
        for copy in copies(c):
            copy.wait_recv()
        wrap = pl.ds(columns, LANES)
        main = pl.ds(0, columns)
        for f in (c, c + 1):
            for j in range(rows // LANES):
                turned = halo[f, :, pl.ds((j + 1) * LANES, LANES)].T
                field[f, pl.ds(HALO + j * LANES, LANES), wrap] = turned * side[:1]
            field[f, pl.ds(0, 8), wrap] = halo[f, :, tile0].T[LANES - 8:] * (side * above)
            field[f, pl.ds(bottom, 8), wrap] = halo[f, :, tile3].T[:8] * (side * below)
            field[f, pl.ds(0, 8), main] = field[f, pl.ds(0, 8), main] * above
            field[f, pl.ds(bottom, 8), main] = field[f, pl.ds(bottom, 8), main] * below

    for f in range(4):
        halo[f, pl.ds(8, LANES - 16), :] = jnp.zeros((LANES - 16, halo.shape[2]), f32)
    offer(0)
    pack(0)
    pl.semaphore_wait(barrier, ndev - 1)
    for copy in copies(0):
        copy.start()
    push(0)
    own = pltpu.make_async_copy(send.at[0, pl.ds(0, MSG), :], recv.at[0, pl.ds(0, MSG), :], self_sem)
    own.start()
    for g in range(1, chunks):
        pack(g)
        push(g)

    shifts = []
    for k in range(1, ndev):
        rest, shift, far = k, [], 0
        for size in (n_gy,) + gx_dims[::-1]:
            shift.append(rest % size)
            far += min(rest % size, size - rest % size)
            rest //= size
        shifts.append((-far, k, shift[0], shift[:0:-1]))
    shifts.sort()

    def sum_copies():
        result = []
        for _, k, dy, dx in shifts:
            to, unit = 0, n_gx
            for size, d in zip(gx_dims, dx):
                unit //= size
                to = to + lax.rem(lax.rem(ix // unit, size) + d, size) * unit
            result.append(
                remote(
                    sums.at[pl.ds(0, 1), :], sums.at[pl.ds(k, 1), :], ar_send, ar_recv, (to, lax.rem(iy + dy, n_gy))
                )
            )
        return result

    def add_all(terms):
        terms = list(terms) + [jnp.zeros((1, LANES), f32)] * (8 - len(terms))
        totals = jnp.sum(jnp.concatenate(terms, axis=0), axis=1, keepdims=True)
        totals = jnp.where(iota((8, LANES), 0) == iota((8, LANES), 1), totals, 0.0)
        sums[pl.ds(0, 1), :] = jnp.sum(totals, axis=0, keepdims=True)
        for copy in sum_copies():
            copy.start()
        others = sums.at[pl.ds(1, ndev - 1), :]
        pltpu.make_async_copy(others, others, ar_recv).wait()
        return jnp.sum(sums[...], axis=0, keepdims=True)

    tiles = (rows + 2 * HALO) // 8
    width = columns + LANES

    def east(x):
        return pltpu.roll(x, width - 1, 1)

    def west(x):
        return pltpu.roll(x, 1, 1)

    sub = iota((8, width), 0)

    def south(x, following):
        return pltpu.roll(jnp.where(sub == 0, following, x), 7, 0)

    def north(x, previous):
        return pltpu.roll(jnp.where(sub == 7, previous, x), 1, 0)

    def tile_at(t):
        if isinstance(t, int):
            return pl.ds(t * 8, 8)
        return pl.ds(pl.multiple_of(t * 8, 8), 8)

    accept(0)

    def node_tile(t, carry):
        here = field[0, tile_at(t), :]
        following = field[0, tile_at(jnp.minimum(t + 1, tiles - 1)), :]
        pair = here + south(here, following)
        nodes[tile_at(t), :] = 0.5 * (pair + east(pair))
        return carry

    lax.fori_loop(0, tiles, node_tile, 0, unroll=2)

    lane16 = iota((16, LANES), 1) // CAP
    sub16 = iota((16, LANES), 0)
    own.wait()
    shift_sum = jnp.zeros((16, LANES), f32)
    for g in range(chunks):
        lo = 1 if g == 0 else 0
        got = recv.at[pl.ds(g * chunk + lo, chunk - lo), pl.ds(0, MSG), :]
        pltpu.make_async_copy(got, got, a2a_recv.at[g]).wait()
        for h in range(chunk // 16):
            base = g * chunk + h * 16
            info = recv[pl.ds(base, 16), 32, :]
            shift_sum = shift_sum + info
            info = jnp.where(sub16 < 8, info, pltpu.roll(info, 64, 1))
            off = jnp.sum(jnp.where(lane16 == sub16, info, 0.0), axis=0, keepdims=True).astype(i32)
            row_hot = (iota((rows, LANES), 0) == lax.shift_right_logical(off, 9)).astype(bf16)
            col = jnp.broadcast_to(lax.bitwise_and(off, 511).astype(f32), (LANES, LANES)).T.astype(i32)
            lane = iota((LANES, LANES), 1)
            shift = lax.bitwise_and(col, LANES - 1)
            index = lax.bitwise_and(lane - shift, LANES - 1)
            lag = lax.shift_right_logical(col, 7) + (lane < shift).astype(i32)
            spread = []
            for c in range(2):
                ab = []
                for half in range(2):
                    x = recv[pl.ds(base, 16), pl.ds((half * 2 + c) * CAP, CAP), :].reshape(LANES, LANES)
                    ab.append(jnp.take_along_axis(x, index, axis=1, mode="promise_in_bounds"))
                for t in range(4):
                    spread.append(
                        jnp.where(lag == t, ab[0], jnp.where(lag == t - 1, ab[1], 0.0))
                    )
            pieces = split3(jnp.concatenate(spread, axis=1))
            add = jnp.dot(
                jnp.concatenate([row_hot] * 3, axis=1), jnp.concatenate(pieces, axis=0), preferred_element_type=f32
            )
            if g == 0 and h == 0:
                deposit[...] = add
            elif g < chunks - 1 or h < chunk // 16 - 1:
                deposit[...] += add
            else:
                add = deposit[...] + add
                field[2, pl.ds(HALO, rows), pl.ds(0, columns)] = add[:, :columns]
                field[3, pl.ds(HALO, rows), pl.ds(0, columns)] = add[:, columns:]
    if chunks * (chunk // 16) == 1:
        field[2, pl.ds(HALO, rows), pl.ds(0, columns)] = deposit[:, :columns]
        field[3, pl.ds(HALO, rows), pl.ds(0, columns)] = deposit[:, columns:]

    sigma = jnp.sum(shift_sum, axis=0, keepdims=True)[:, 64:65] * (1.0 / (ndev * GRAIN))
    offer(2)
    for copy in copies(2):
        copy.start()
    accept(2)

    def fold(x):
        return sum(x[:, k * LANES:(k + 1) * LANES] for k in range(columns // LANES))

    def apply(source, target, products):
        su, sv = source
        tu, tv = target

        def step(t, carry, mask, count_it):
            syy_old, sxy_old, acc = carry
            nxt = min(t + 1, tiles - 1) if isinstance(t, int) else t + 1
            here, there = tile_at(t), tile_at(nxt)
            u, v = su[here, :], sv[here, :]
            us, vs = south(u, su[there, :]), south(v, sv[there, :])
            s = nodes[here, :]
            exx = east(u) - u
            eyy = vs - v
            both = exx + eyy
            sxx = s * (exx + both)
            syy = s * (eyy + both)
            sxy = (0.5 * s) * ((us - u) + (east(v) - v))
            drag = field[1, here, :] - sigma
            au = (west(sxx) - sxx) + (north(sxy, sxy_old) - sxy) + drag * u
            av = (north(syy, syy_old) - syy) + (west(sxy) - sxy) + drag * v
            au = au * mask
            av = av * mask
            tu[here, :] = au
            tv[here, :] = av
            if count_it:
                acc = tuple(
                    a + fold(p[0] * q[0] + p[1] * q[1])
                    for a, (p, q) in zip(acc, [(((u, v), (au, av))[i], ((u, v), (au, av))[j]) for i, j in products])
                )
            return syy, sxy, acc

        zero = jnp.zeros((8, width), f32)
        carry = (zero, zero, tuple(jnp.zeros((8, LANES), f32) for _ in products))
        carry = step(0, carry, mask_main * above, False)
        carry = lax.fori_loop(1, tiles - 1, lambda t, c: step(t, c, mask_main, True), carry, unroll=8)
        carry = step(tiles - 1, carry, mask_main * below, False)
        return [jnp.sum(a, axis=0, keepdims=True) for a in carry[2]]

    f0 = (field.at[2], field.at[3])
    f1, f2, f3 = ((q.at[0], q.at[1]) for q in (q1, q2, q3))
    terms = apply(f0, f1, ((0, 0), (0, 1), (1, 1)))
    terms += apply(f1, f2, ((0, 1), (1, 1)))
    terms += apply(f2, f3, ((0, 1),))
    products = add_all(terms)

    m = [products[:, k:k + 1] / products[:, :1] for k in range(6)]

    def form(a, shifted):
        result = 0.0
        for i in range(len(a)):
            for j in range(i, len(a)):
                w = m[i + j + 1] + sigma * m[i + j] if shifted else m[i + j]
                term = a[i] * a[j] * w
                result = result + (term if i == j else 2.0 * term)
        return result

    one = jnp.ones((1, 1), f32)
    d, r, x, rr = [one], [one], [0.0 * one] * 3, one
    for k in range(3):
        alpha = rr / form(d, True)
        x = [x[i] + alpha * d[i] if i < len(d) else x[i] for i in range(3)]
        image = [sigma * d[i] for i in range(len(d))] + [0.0 * one]
        image = [image[i] + d[i - 1] if i else image[i] for i in range(len(image))]
        r = [(r[i] if i < len(r) else 0.0) - alpha * image[i] for i in range(len(image))]
        if k < 2:
            fresh = form(r, False)
            beta = fresh / rr
            d = [r[i] + (beta * d[i] if i < len(d) else 0.0) for i in range(len(r))]
            rr = fresh

    def finish(t, carry):
        here = pl.ds(pl.multiple_of(t * 8, 8), 8)
        padded = pl.ds(pl.multiple_of(t * 8 + HALO, 8), 8)
        main = pl.ds(0, columns)
        for c in range(2):
            a0, a1, a2, a3 = field[2 + c, padded, main], q1[c, padded, main], q2[c, padded, main], q3[c, padded, main]
            out_x[c, here, :] = x[0] * a0 + x[1] * a1 + x[2] * a2
            out_r[c, here, :] = r[0] * a0 + r[1] * a1 + r[2] * a2 + r[3] * a3
        return carry

    lax.fori_loop(0, rows // 8, finish, 0, unroll=4)

    for c in (0, 2):
        for copy in copies(c):
            copy.wait_send()
    others = sums.at[pl.ds(1, ndev - 1), :]
    pltpu.make_async_copy(others, others, ar_send).wait()
    for g in range(chunks):
        lo = 1 if g == 0 else 0
        sent = send.at[pl.ds(g * chunk + lo, chunk - lo), pl.ds(0, MSG), :]
        pltpu.make_async_copy(sent, sent, a2a_send.at[g]).wait()


def shards(n_gx, n_gy, misfit, owners, offsets, counts, viscosity, friction):
    ndev = n_gx * n_gy
    slots = owners.shape[0]
    rows, columns = viscosity.shape
    chunk = min(32, ndev)
    chunks = ndev // chunk
    padded = (rows + 2 * HALO, columns + LANES)
    pixels = misfit.reshape(slots, 2, 2, LANES).transpose(0, 2, 1, 3).reshape(slots * 4, LANES)
    vmem = pl.BlockSpec(memory_space=pltpu.VMEM)
    hbm = pl.BlockSpec(memory_space=pltpu.HBM)
    smem = pl.BlockSpec(memory_space=pltpu.SMEM)
    out = jax.ShapeDtypeStruct((2, rows, columns), f32)
    dma = pltpu.SemaphoreType.DMA
    return pl.pallas_call(
        functools.partial(kernel, n_gx, n_gy, chunk),
        out_shape=(out, out),
        in_specs=[hbm, hbm, hbm, smem, hbm, hbm],
        out_specs=(vmem, vmem),
        scratch_shapes=[
            pltpu.VMEM((slots * 4, LANES), f32),
            pltpu.VMEM((slots // LANES, LANES), i32),
            pltpu.VMEM((slots // LANES, LANES), i32),
            pltpu.VMEM((slots, 12 * LANES), bf16),
            pltpu.VMEM((ndev, PAD, LANES), f32),
            pltpu.VMEM((ndev, PAD, LANES), f32),
            pltpu.VMEM((rows, 2 * columns), f32),
            pltpu.VMEM((4,) + padded, f32),
            pltpu.VMEM(padded, f32),
            pltpu.VMEM((2,) + padded, f32),
            pltpu.VMEM((2,) + padded, f32),
            pltpu.VMEM((2,) + padded, f32),
            pltpu.VMEM((4, LANES, rows), f32),
            pltpu.VMEM((4, LANES, rows + 2 * LANES), f32),
            pltpu.VMEM((ndev, LANES), f32),
            dma((5,)),
            dma((chunks,)),
            dma((chunks,)),
            dma,
            dma((2, 8)),
            dma((2, 8)),
            dma,
            dma,
        ],
        compiler_params=pltpu.CompilerParams(
            collective_id=0, has_side_effects=True, vmem_limit_bytes=54 * 1024 * 1024
        ),
    )(
        pixels,
        owners.reshape(slots // LANES, LANES),
        offsets.reshape(slots // LANES, LANES),
        counts,
        viscosity,
        friction,
    )


def solution(mesh):
    in_specs = (
        P(("gx", "gy"), None, None),
        P(("gx", "gy")),
        P(("gx", "gy")),
        P(("gx", "gy")),
        P("gy", "gx"),
        P("gy", "gx"),
    )
    out_specs = (P(None, "gy", "gx"), P(None, "gy", "gx"))
    return jax.shard_map(
        functools.partial(shards, mesh.shape["gx"], mesh.shape["gy"]),
        mesh=mesh, in_specs=in_specs, out_specs=out_specs, check_vma=False,
    )
```

```python
import functools

import jax
import jax.numpy as jnp
import numpy as np
from jax import lax
from jax.experimental import pallas as pl
from jax.experimental.pallas import tpu as pltpu
from jax.sharding import PartitionSpec as P

MESH = pl.DeviceIdType.MESH
CAP = 8
LANES = 128
HALO = 8
MSG = 33
PAD = 40
GRAIN = 1024.0
bf16, f32, i32 = jnp.bfloat16, jnp.float32, jnp.int32


def split3(x):
    hi = x.astype(bf16)
    rest = x - hi.astype(f32)
    mid = rest.astype(bf16)
    low = (rest - mid.astype(f32)).astype(bf16)
    return hi, mid, low


def iota(shape, dim):
    return lax.broadcasted_iota(i32, shape, dim)


def remote(src, dst, send_sem, recv_sem, dev):
    return pltpu.make_async_remote_copy(
        src_ref=src, dst_ref=dst, send_sem=send_sem, recv_sem=recv_sem, device_id=dev, device_id_type=MESH
    )


def plan(n_gx, n_gy):
    sizes = ((4, 4, 2) if n_gx == 32 else (n_gx // 2, 2)) + (n_gy,)
    ndev = n_gx * n_gy
    shifts = []
    for p in range(1, ndev):
        rest, shift = p * 37 % ndev, []
        for size in sizes[::-1]:
            shift.insert(0, rest % size)
            rest //= size
        shifts.append(tuple(shift))

    def hops(shift):
        return sum(min(d, n - d) for d, n in zip(shift[:-2] + shift[-1:], sizes[:-2] + sizes[-1:]))

    near = sorted(shifts, key=lambda s: -hops(s))[-30 * ndev // 128:]
    order = [(0,) * len(sizes)] + [s for s in shifts if s not in near] + near
    return sizes, order, sorted(shifts, key=lambda s: -hops(s))


def code(shift, sizes):
    result = 0
    for d, n in zip(shift, sizes):
        result = result * n + d
    return result


def kernel(
    n_gx, n_gy, chunk,
    misfit_hbm, owners_hbm, offsets_hbm, counts, viscosity_hbm, friction_hbm, codes_hbm, basis, weights_out,
    misfit, owners, offsets, codes, parts, send, recv, deposit, field, nodes, q1, q2, q3, strips, halo, sums,
    in_sem, out_sem, a2a_send, a2a_recv, self_sem, ex_send, ex_recv, ar_send, ar_recv,
):
    ndev = n_gx * n_gy
    ix, iy = lax.axis_index("gx"), lax.axis_index("gy")
    me = ix * n_gy + iy
    slots = misfit.shape[0] // 4
    rows, columns = viscosity_hbm.shape
    chunks = ndev // chunk
    keys = chunk * CAP
    sizes, order, farthest = plan(n_gx, n_gy)

    def split(x, y):
        result, unit = [], n_gx
        for n in sizes[:-1]:
            unit //= n
            result.append(lax.rem(x // unit, n))
        return result + [y]

    here = split(ix, iy)

    def peer(shift):
        at = [lax.rem(a + d, n) for a, d, n in zip(here, shift, sizes)]
        return code(at[:-1], sizes[:-1]), at[-1]

    loads = [
        pltpu.make_async_copy(src, dst, in_sem.at[k])
        for k, (src, dst) in enumerate(
            (
                (owners_hbm, owners),
                (offsets_hbm, offsets),
                (codes_hbm, codes),
                (viscosity_hbm, field.at[0, pl.ds(HALO, rows), pl.ds(0, columns)]),
                (friction_hbm, field.at[1, pl.ds(HALO, rows), pl.ds(0, columns)]),
                (misfit_hbm, misfit),
            )
        )
    ]
    for load in loads:
        load.start()
    barrier = pltpu.get_barrier_semaphore()
    for shift in farthest:
        pl.semaphore_signal(barrier, inc=1, device_id=peer(shift), device_id_type=MESH)

    for load in loads[:3]:
        load.wait()

    count = counts[0]
    lane_blocks = slots // LANES
    upper = (iota((LANES, LANES), 0) < iota((LANES, LANES), 1)).astype(bf16)
    carry = jnp.zeros((ndev, 1), f32)
    hots, targets, weights = [], [], []
    for b in range(lane_blocks):
        own = owners[pl.ds(b, 1), :]
        off = offsets[pl.ds(b, 1), :]
        live = (iota((1, LANES), 1) + b * LANES) < count
        theirs = split(own // n_gy, lax.rem(own, n_gy))
        rel = code([lax.rem(a - b + n, n) for a, b, n in zip(theirs, here, sizes)], sizes)
        hot = (codes[:, :LANES] == jnp.where(live, rel, -1)).astype(f32)
        number = jnp.sum(hot * iota((ndev, LANES), 0).astype(f32), axis=0, keepdims=True).astype(i32)
        before = jnp.dot(hot.astype(bf16), upper, preferred_element_type=f32) + carry
        rank = jnp.sum(hot * before, axis=0, keepdims=True).astype(i32)
        carry = carry + jnp.sum(hot, axis=1, keepdims=True)
        targets.append(jnp.where(live, number * CAP + rank, -1))
        hots.append(hot.astype(bf16))
        mine = lax.rem(iota((LANES, LANES), 0), CAP) == rank
        row_part = jnp.where(mine, lax.shift_right_logical(off, 9).astype(f32), 0.0)
        col_part = jnp.where(mine, lax.bitwise_and(off, 511).astype(f32), 0.0)
        weights.append(jnp.concatenate([row_part, col_part], axis=0).astype(bf16))
    target = jnp.concatenate(targets, axis=1)
    hot = jnp.concatenate(hots, axis=1)
    weight = jnp.concatenate(weights, axis=1)
    meta = lax.dot_general(hot, weight, (((1,), (1,)), ((), ())), preferred_element_type=f32)
    meta = meta[:, :LANES] * 512.0 + meta[:, LANES:]

    loads[3].wait()
    loads[4].wait()

    def share_tile(t, total):
        at = pl.ds(pl.multiple_of(t * 8 + HALO, 8), 8)
        return total + 10.0 * field[0, at, pl.ds(0, columns)] + field[1, at, pl.ds(0, columns)]

    share = lax.fori_loop(0, rows // 8, share_tile, jnp.zeros((8, columns), f32), unroll=4)
    share = jnp.sum(jnp.sum(share, axis=0, keepdims=True), axis=1, keepdims=True)
    share = jnp.round(share * (GRAIN / (rows * columns)))
    send[:, 32, :] = jnp.where(iota((ndev, LANES), 1) < 64, meta, share)

    loads[5].wait()
    for t in range(4):
        hi, mid, low = split3(misfit[pl.ds(t, slots, stride=4), :])
        parts[:, pl.ds(t * LANES, LANES)] = hi
        parts[:, pl.ds((4 + t) * LANES, LANES)] = mid
        parts[:, pl.ds((8 + t) * LANES, LANES)] = low

    def pack(g):
        place = ((iota((keys, slots), 0) + g * keys) == target).astype(bf16)
        packed = jnp.dot(place, parts[...], preferred_element_type=f32)
        packed = packed[:, :512] + packed[:, 512:1024] + packed[:, 1024:]
        for t in range(4):
            send[pl.ds(g * chunk, chunk), pl.ds(t * CAP, CAP), :] = packed[:, t * LANES:(t + 1) * LANES].reshape(
                chunk, CAP, LANES
            )

    def push(g):
        for p in range(max(g * chunk, 1), (g + 1) * chunk):
            remote(
                send.at[p, pl.ds(0, MSG), :], recv.at[p, pl.ds(0, MSG), :], a2a_send.at[g], a2a_recv.at[g], peer(order[p])
            ).start()

    left, right = lax.rem(ix + n_gx - 1, n_gx), lax.rem(ix + 1, n_gx)
    up, down = lax.rem(iy + n_gy - 1, n_gy), lax.rem(iy + 1, n_gy)
    bottom = HALO + rows
    first, last = pl.ds(0, 8), pl.ds(LANES - 8, 8)
    tile0, tile3 = pl.ds(0, LANES), pl.ds(LANES + rows, LANES)
    part0, part1, whole = pl.ds(0, LANES), pl.ds(rows - LANES, LANES), pl.ds(0, rows)
    lane_tile = iota((8, LANES), 1)
    side = jnp.where(lane_tile < 64, jnp.where(ix < n_gx - 1, 1.0, 0.0), jnp.where(ix > 0, 1.0, 0.0))
    above = jnp.where(iy > 0, 1.0, 0.0)
    below = jnp.where(iy < n_gy - 1, 1.0, 0.0)
    mask_main = jnp.concatenate([jnp.ones((8, columns), f32), side], axis=1)

    def copies(c):
        pair = pl.ds(c, 2)
        main = pl.ds(0, columns)
        moves = (
            (field.at[pair, pl.ds(HALO, 8), main], field.at[pair, pl.ds(bottom, 8), main], (ix, up)),
            (field.at[pair, pl.ds(bottom - 8, 8), main], field.at[pair, pl.ds(0, 8), main], (ix, down)),
            (strips.at[pair, first, whole], halo.at[pair, first, pl.ds(LANES, rows)], (left, iy)),
            (strips.at[pair, last, whole], halo.at[pair, last, pl.ds(LANES, rows)], (right, iy)),
            (strips.at[pair, first, part0], halo.at[pair, first, tile3], (left, up)),
            (strips.at[pair, first, part1], halo.at[pair, first, tile0], (left, down)),
            (strips.at[pair, last, part0], halo.at[pair, last, tile3], (right, up)),
            (strips.at[pair, last, part1], halo.at[pair, last, tile0], (right, down)),
        )
        h = c // 2
        return [remote(s, d, ex_send.at[h, k], ex_recv.at[h, k], dev) for k, (s, d, dev) in enumerate(moves)]

    def offer(c):
        for f in (c, c + 1):
            for j in range(rows // LANES):
                at = pl.ds(HALO + j * LANES, LANES)
                mix = jnp.where(
                    iota((LANES, LANES), 1) < 64, field[f, at, pl.ds(0, LANES)], field[f, at, pl.ds(columns - LANES, LANES)]
                )
                strips[f, :, pl.ds(j * LANES, LANES)] = mix.T

    def accept(c):
        for copy in copies(c):
            copy.wait_recv()
        wrap = pl.ds(columns, LANES)
        main = pl.ds(0, columns)
        for f in (c, c + 1):
            for j in range(rows // LANES):
                turned = halo[f, :, pl.ds((j + 1) * LANES, LANES)].T
                field[f, pl.ds(HALO + j * LANES, LANES), wrap] = turned * side[:1]
            field[f, pl.ds(0, 8), wrap] = halo[f, :, tile0].T[LANES - 8:] * (side * above)
            field[f, pl.ds(bottom, 8), wrap] = halo[f, :, tile3].T[:8] * (side * below)
            field[f, pl.ds(0, 8), main] = field[f, pl.ds(0, 8), main] * above
            field[f, pl.ds(bottom, 8), main] = field[f, pl.ds(bottom, 8), main] * below

    for f in range(4):
        halo[f, pl.ds(8, LANES - 16), :] = jnp.zeros((LANES - 16, halo.shape[2]), f32)
    pack(0)
    pl.semaphore_wait(barrier, ndev - 1)
    push(0)
    offer(0)
    for copy in copies(0):
        copy.start()
    own = pltpu.make_async_copy(send.at[0, pl.ds(0, MSG), :], recv.at[0, pl.ds(0, MSG), :], self_sem)
    own.start()
    for g in range(1, chunks):
        pack(g)
        push(g)

    def sum_copies():
        return [
            remote(sums.at[pl.ds(0, 1), :], sums.at[pl.ds(k, 1), :], ar_send, ar_recv, peer(shift))
            for k, shift in enumerate(farthest, 1)
        ]

    def add_all(terms):
        terms = list(terms) + [jnp.zeros((1, LANES), f32)] * (8 - len(terms))
        totals = jnp.sum(jnp.concatenate(terms, axis=0), axis=1, keepdims=True)
        totals = jnp.where(iota((8, LANES), 0) == iota((8, LANES), 1), totals, 0.0)
        sums[pl.ds(0, 1), :] = jnp.sum(totals, axis=0, keepdims=True)
        for copy in sum_copies():
            copy.start()
        others = sums.at[pl.ds(1, ndev - 1), :]
        pltpu.make_async_copy(others, others, ar_recv).wait()
        return jnp.sum(sums[...], axis=0, keepdims=True)

    tiles = (rows + 2 * HALO) // 8
    width = columns + LANES

    def east(x):
        return pltpu.roll(x, width - 1, 1)

    def west(x):
        return pltpu.roll(x, 1, 1)

    sub = iota((8, width), 0)

    def south(x, following):
        return pltpu.roll(jnp.where(sub == 0, following, x), 7, 0)

    def north(x, previous):
        return pltpu.roll(jnp.where(sub == 7, previous, x), 1, 0)

    def tile_at(t):
        if isinstance(t, int):
            return pl.ds(t * 8, 8)
        return pl.ds(pl.multiple_of(t * 8, 8), 8)

    accept(0)

    def node_tile(t, carry):
        here = field[0, tile_at(t), :]
        following = field[0, tile_at(jnp.minimum(t + 1, tiles - 1)), :]
        pair = here + south(here, following)
        nodes[tile_at(t), :] = 0.5 * (pair + east(pair))
        return carry

    lax.fori_loop(0, tiles, node_tile, 0, unroll=2)

    lane16 = iota((16, LANES), 1) // CAP
    sub16 = iota((16, LANES), 0)
    own.wait()
    shift_sum = jnp.zeros((16, LANES), f32)
    for g in range(chunks):
        lo = 1 if g == 0 else 0
        got = recv.at[pl.ds(g * chunk + lo, chunk - lo), pl.ds(0, MSG), :]
        pltpu.make_async_copy(got, got, a2a_recv.at[g]).wait()
        for h in range(chunk // 16):
            base = g * chunk + h * 16
            info = recv[pl.ds(base, 16), 32, :]
            shift_sum = shift_sum + info
            info = jnp.where(sub16 < 8, info, pltpu.roll(info, 64, 1))
            off = jnp.sum(jnp.where(lane16 == sub16, info, 0.0), axis=0, keepdims=True).astype(i32)
            row_hot = (iota((rows, LANES), 0) == lax.shift_right_logical(off, 9)).astype(bf16)
            col = jnp.broadcast_to(lax.bitwise_and(off, 511).astype(f32), (LANES, LANES)).T.astype(i32)
            lane = iota((LANES, LANES), 1)
            shift = lax.bitwise_and(col, LANES - 1)
            index = lax.bitwise_and(lane - shift, LANES - 1)
            lag = lax.shift_right_logical(col, 7) + (lane < shift).astype(i32)
            spread = []
            for c in range(2):
                ab = []
                for half in range(2):
                    x = recv[pl.ds(base, 16), pl.ds((half * 2 + c) * CAP, CAP), :].reshape(LANES, LANES)
                    ab.append(jnp.take_along_axis(x, index, axis=1, mode="promise_in_bounds"))
                for t in range(4):
                    spread.append(
                        jnp.where(lag == t, ab[0], jnp.where(lag == t - 1, ab[1], 0.0))
                    )
            pieces = split3(jnp.concatenate(spread, axis=1))
            add = jnp.dot(
                jnp.concatenate([row_hot] * 3, axis=1), jnp.concatenate(pieces, axis=0), preferred_element_type=f32
            )
            if g == 0 and h == 0:
                deposit[...] = add
            elif g < chunks - 1 or h < chunk // 16 - 1:
                deposit[...] += add
            else:
                add = deposit[...] + add
                field[2, pl.ds(HALO, rows), pl.ds(0, columns)] = add[:, :columns]
                field[3, pl.ds(HALO, rows), pl.ds(0, columns)] = add[:, columns:]
    if chunks * (chunk // 16) == 1:
        field[2, pl.ds(HALO, rows), pl.ds(0, columns)] = deposit[:, :columns]
        field[3, pl.ds(HALO, rows), pl.ds(0, columns)] = deposit[:, columns:]

    sigma = jnp.sum(shift_sum, axis=0, keepdims=True)[:, 64:65] * (1.0 / (ndev * GRAIN))
    offer(2)
    for copy in copies(2):
        copy.start()
    accept(2)

    def fold(x):
        return sum(x[:, k * LANES:(k + 1) * LANES] for k in range(columns // LANES))

    def apply(source, target, products):
        su, sv = source
        tu, tv = target

        def step(t, carry, mask, count_it):
            syy_old, sxy_old, acc = carry
            nxt = min(t + 1, tiles - 1) if isinstance(t, int) else t + 1
            here, there = tile_at(t), tile_at(nxt)
            u, v = su[here, :], sv[here, :]
            us, vs = south(u, su[there, :]), south(v, sv[there, :])
            s = nodes[here, :]
            exx = east(u) - u
            eyy = vs - v
            both = exx + eyy
            sxx = s * (exx + both)
            syy = s * (eyy + both)
            sxy = (0.5 * s) * ((us - u) + (east(v) - v))
            drag = field[1, here, :] - sigma
            au = (west(sxx) - sxx) + (north(sxy, sxy_old) - sxy) + drag * u
            av = (north(syy, syy_old) - syy) + (west(sxy) - sxy) + drag * v
            au = au * mask
            av = av * mask
            tu[here, :] = au
            tv[here, :] = av
            if count_it:
                acc = tuple(
                    a + fold(p[0] * q[0] + p[1] * q[1])
                    for a, (p, q) in zip(acc, [(((u, v), (au, av))[i], ((u, v), (au, av))[j]) for i, j in products])
                )
            return syy, sxy, acc

        zero = jnp.zeros((8, width), f32)
        carry = (zero, zero, tuple(jnp.zeros((8, LANES), f32) for _ in products))
        carry = step(0, carry, mask_main * above, False)
        carry = lax.fori_loop(1, tiles - 1, lambda t, c: step(t, c, mask_main, True), carry, unroll=8)
        carry = step(tiles - 1, carry, mask_main * below, False)
        return [jnp.sum(a, axis=0, keepdims=True) for a in carry[2]]

    f0 = (field.at[2], field.at[3])
    f1, f2, f3 = ((q.at[0], q.at[1]) for q in (q1, q2, q3))
    terms = apply(f0, f1, ((0, 0), (0, 1), (1, 1)))
    terms += apply(f1, f2, ((0, 1), (1, 1)))
    terms += apply(f2, f3, ((0, 1),))
    saves = [
        pltpu.make_async_copy(src.at[pl.ds(at, 2), pl.ds(HALO, rows), pl.ds(0, columns)], basis.at[k], out_sem.at[k])
        for k, (src, at) in enumerate(((field, 2), (q1, 0), (q2, 0), (q3, 0)))
    ]
    for save in saves:
        save.start()
    products = add_all(terms)

    m = [products[:, k:k + 1] / products[:, :1] for k in range(6)]

    def form(a, shifted):
        result = 0.0
        for i in range(len(a)):
            for j in range(i, len(a)):
                w = m[i + j + 1] + sigma * m[i + j] if shifted else m[i + j]
                term = a[i] * a[j] * w
                result = result + (term if i == j else 2.0 * term)
        return result

    one = jnp.ones((1, 1), f32)
    d, r, x, rr = [one], [one], [0.0 * one] * 3, one
    for k in range(3):
        alpha = rr / form(d, True)
        x = [x[i] + alpha * d[i] if i < len(d) else x[i] for i in range(3)]
        image = [sigma * d[i] for i in range(len(d))] + [0.0 * one]
        image = [image[i] + d[i - 1] if i else image[i] for i in range(len(image))]
        r = [(r[i] if i < len(r) else 0.0) - alpha * image[i] for i in range(len(image))]
        if k < 2:
            fresh = form(r, False)
            beta = fresh / rr
            d = [r[i] + (beta * d[i] if i < len(d) else 0.0) for i in range(len(r))]
            rr = fresh

    weights_out[...] = jnp.concatenate([jnp.broadcast_to(w, (1, LANES)) for w in x + r + [one]], axis=0)
    for save in saves:
        save.wait()

    for c in (0, 2):
        for copy in copies(c):
            copy.wait_send()
    others = sums.at[pl.ds(1, ndev - 1), :]
    pltpu.make_async_copy(others, others, ar_send).wait()
    for g in range(chunks):
        lo = 1 if g == 0 else 0
        sent = send.at[pl.ds(g * chunk + lo, chunk - lo), pl.ds(0, MSG), :]
        pltpu.make_async_copy(sent, sent, a2a_send.at[g]).wait()


def combine(weights, basis, out_x, out_r):
    w = [weights[k:k + 1, :1] for k in range(7)]
    for c in range(2):
        a0, a1, a2, a3 = (basis[k, c] for k in range(4))
        out_x[c] = w[0] * a0 + w[1] * a1 + w[2] * a2
        out_r[c] = w[3] * a0 + w[4] * a1 + w[5] * a2 + w[6] * a3


def shards(n_gx, n_gy, misfit, owners, offsets, counts, viscosity, friction):
    ndev = n_gx * n_gy
    slots = owners.shape[0]
    rows, columns = viscosity.shape
    chunk = min(32, ndev)
    chunks = ndev // chunk
    padded = (rows + 2 * HALO, columns + LANES)
    pixels = misfit.reshape(slots, 2, 2, LANES).transpose(0, 2, 1, 3).reshape(slots * 4, LANES)
    vmem = pl.BlockSpec(memory_space=pltpu.VMEM)
    hbm = pl.BlockSpec(memory_space=pltpu.HBM)
    smem = pl.BlockSpec(memory_space=pltpu.SMEM)
    out = jax.ShapeDtypeStruct((2, rows, columns), f32)
    sizes, order, _ = plan(n_gx, n_gy)
    codes = np.tile(np.array([[code(s, sizes)] for s in order], np.int32), (1, LANES))
    dma = pltpu.SemaphoreType.DMA
    basis, weights = pl.pallas_call(
        functools.partial(kernel, n_gx, n_gy, chunk),
        out_shape=(jax.ShapeDtypeStruct((4, 2, rows, columns), f32), jax.ShapeDtypeStruct((8, LANES), f32)),
        in_specs=[hbm, hbm, hbm, smem, hbm, hbm, hbm],
        out_specs=(hbm, vmem),
        scratch_shapes=[
            pltpu.VMEM((slots * 4, LANES), f32),
            pltpu.VMEM((slots // LANES, LANES), i32),
            pltpu.VMEM((slots // LANES, LANES), i32),
            pltpu.VMEM((ndev, LANES), i32),
            pltpu.VMEM((slots, 12 * LANES), bf16),
            pltpu.VMEM((ndev, PAD, LANES), f32),
            pltpu.VMEM((ndev, PAD, LANES), f32),
            pltpu.VMEM((rows, 2 * columns), f32),
            pltpu.VMEM((4,) + padded, f32),
            pltpu.VMEM(padded, f32),
            pltpu.VMEM((2,) + padded, f32),
            pltpu.VMEM((2,) + padded, f32),
            pltpu.VMEM((2,) + padded, f32),
            pltpu.VMEM((4, LANES, rows), f32),
            pltpu.VMEM((4, LANES, rows + 2 * LANES), f32),
            pltpu.VMEM((ndev, LANES), f32),
            dma((6,)),
            dma((4,)),
            dma((chunks,)),
            dma((chunks,)),
            dma,
            dma((2, 8)),
            dma((2, 8)),
            dma,
            dma,
        ],
        compiler_params=pltpu.CompilerParams(
            collective_id=0, has_side_effects=True, vmem_limit_bytes=54 * 1024 * 1024
        ),
    )(
        pixels,
        owners.reshape(slots // LANES, LANES),
        offsets.reshape(slots // LANES, LANES),
        counts,
        viscosity,
        friction,
        codes,
    )
    block = min(128, rows)
    spec = pl.BlockSpec((2, block, columns), lambda i: (0, i, 0))
    return pl.pallas_call(
        combine,
        out_shape=(out, out),
        grid=(rows // block,),
        in_specs=[pl.BlockSpec((8, LANES), lambda i: (0, 0)), pl.BlockSpec((4, 2, block, columns), lambda i: (0, 0, i, 0))],
        out_specs=(spec, spec),
    )(weights, basis)


def solution(mesh):
    in_specs = (
        P(("gx", "gy"), None, None),
        P(("gx", "gy")),
        P(("gx", "gy")),
        P(("gx", "gy")),
        P("gy", "gx"),
        P("gy", "gx"),
    )
    out_specs = (P(None, "gy", "gx"), P(None, "gy", "gx"))
    return jax.shard_map(
        functools.partial(shards, mesh.shape["gx"], mesh.shape["gy"]),
        mesh=mesh, in_specs=in_specs, out_specs=out_specs, check_vma=False,
    )
```

```python
import functools

import jax
import jax.numpy as jnp
import numpy as np
from jax import lax
from jax.experimental import pallas as pl
from jax.experimental.pallas import tpu as pltpu
from jax.sharding import PartitionSpec as P

MESH = pl.DeviceIdType.MESH
CAP = 8
LANES = 128
HALO = 8
MSG = 33
PAD = 40
GRAIN = 1024.0
bf16, f32, i32 = jnp.bfloat16, jnp.float32, jnp.int32


def split3(x):
    hi = x.astype(bf16)
    rest = x - hi.astype(f32)
    mid = rest.astype(bf16)
    low = (rest - mid.astype(f32)).astype(bf16)
    return hi, mid, low


def iota(shape, dim):
    return lax.broadcasted_iota(i32, shape, dim)


def remote(src, dst, send_sem, recv_sem, dev):
    return pltpu.make_async_remote_copy(
        src_ref=src, dst_ref=dst, send_sem=send_sem, recv_sem=recv_sem, device_id=dev, device_id_type=MESH
    )


def plan(n_gx, n_gy):
    sizes = ((4, 4, 2) if n_gx == 32 else (n_gx // 2, 2)) + (n_gy,)
    ndev = n_gx * n_gy
    shifts = []
    for p in range(1, ndev):
        rest, shift = p * 37 % ndev, []
        for size in sizes[::-1]:
            shift.insert(0, rest % size)
            rest //= size
        shifts.append(tuple(shift))

    def hops(shift):
        return sum(min(d, n - d) for d, n in zip(shift[:-2] + shift[-1:], sizes[:-2] + sizes[-1:]))

    near = sorted(shifts, key=lambda s: -hops(s))[-30 * ndev // 128:]
    order = [(0,) * len(sizes)] + [s for s in shifts if s not in near] + near
    return sizes, order, sorted(shifts, key=lambda s: -hops(s))


def code(shift, sizes):
    result = 0
    for d, n in zip(shift, sizes):
        result = result * n + d
    return result


def kernel(
    n_gx, n_gy, chunk,
    misfit_hbm, owners_hbm, offsets_hbm, counts_hbm, viscosity_hbm, friction_hbm, codes_hbm, basis, weights_out,
    misfit, owners, offsets, codes, counts, parts, send, recv, deposit, field, nodes, halved, q1, q2, q3, strips, halo, sums,
    in_sem, out_sem, a2a_send, a2a_recv, ex_send, ex_recv, ar_send, ar_recv,
):
    ndev = n_gx * n_gy
    ix, iy = lax.axis_index("gx"), lax.axis_index("gy")
    me = ix * n_gy + iy
    slots = misfit.shape[0] // 4
    rows, columns = viscosity_hbm.shape
    chunks = ndev // chunk
    keys = chunk * CAP
    sizes, order, farthest = plan(n_gx, n_gy)

    def split(x, y):
        result, unit = [], n_gx
        for n in sizes[:-1]:
            unit //= n
            result.append(lax.rem(x // unit, n))
        return result + [y]

    here = split(ix, iy)

    def peer(shift):
        at = [lax.rem(a + d, n) for a, d, n in zip(here, shift, sizes)]
        return code(at[:-1], sizes[:-1]), at[-1]

    loads = [
        pltpu.make_async_copy(src, dst, in_sem.at[k])
        for k, (src, dst) in enumerate(
            (
                (owners_hbm, owners),
                (offsets_hbm, offsets),
                (codes_hbm, codes),
                (counts_hbm, counts),
                (viscosity_hbm, field.at[0, pl.ds(HALO, rows), pl.ds(0, columns)]),
                (friction_hbm, field.at[1, pl.ds(HALO, rows), pl.ds(0, columns)]),
                (misfit_hbm, misfit),
            )
        )
    ]
    for load in loads:
        load.start()
    barrier = pltpu.get_barrier_semaphore()
    for shift in farthest:
        pl.semaphore_signal(barrier, inc=1, device_id=peer(shift), device_id_type=MESH)

    for load in loads[:4]:
        load.wait()

    count = counts[...]
    lane_blocks = slots // LANES
    upper = (iota((LANES, LANES), 0) < iota((LANES, LANES), 1)).astype(bf16)
    carry = jnp.zeros((ndev, 1), f32)
    hots, targets, weights = [], [], []
    for b in range(lane_blocks):
        own = owners[pl.ds(b, 1), :]
        off = offsets[pl.ds(b, 1), :]
        live = (iota((1, LANES), 1) + b * LANES) < count
        theirs = split(own // n_gy, lax.rem(own, n_gy))
        rel = code([lax.rem(a - b + n, n) for a, b, n in zip(theirs, here, sizes)], sizes)
        hot = (codes[:, :LANES] == jnp.where(live, rel, -1)).astype(f32)
        number = jnp.sum(hot * iota((ndev, LANES), 0).astype(f32), axis=0, keepdims=True).astype(i32)
        before = jnp.dot(hot.astype(bf16), upper, preferred_element_type=f32) + carry
        rank = jnp.sum(hot * before, axis=0, keepdims=True).astype(i32)
        carry = carry + jnp.sum(hot, axis=1, keepdims=True)
        targets.append(jnp.where(live, number * CAP + rank, -1))
        hots.append(hot.astype(bf16))
        mine = lax.rem(iota((LANES, LANES), 0), CAP) == rank
        row_part = jnp.where(mine, lax.shift_right_logical(off, 9).astype(f32), 0.0)
        col_part = jnp.where(mine, lax.bitwise_and(off, 511).astype(f32), 0.0)
        weights.append(jnp.concatenate([row_part, col_part], axis=0).astype(bf16))
    target = jnp.concatenate(targets, axis=1)
    hot = jnp.concatenate(hots, axis=1)
    weight = jnp.concatenate(weights, axis=1)
    meta = lax.dot_general(hot, weight, (((1,), (1,)), ((), ())), preferred_element_type=f32)
    meta = meta[:, :LANES] * 512.0 + meta[:, LANES:]

    loads[4].wait()
    loads[5].wait()

    def share_tile(t, total):
        at = pl.ds(pl.multiple_of(t * 8 + HALO, 8), 8)
        return total + 10.0 * field[0, at, pl.ds(0, columns)] + field[1, at, pl.ds(0, columns)]

    share = lax.fori_loop(0, rows // 8, share_tile, jnp.zeros((8, columns), f32), unroll=4)
    share = jnp.sum(jnp.sum(share, axis=0, keepdims=True), axis=1, keepdims=True)
    share = jnp.round(share * (GRAIN / (rows * columns)))
    send[:, 32, :] = jnp.where(iota((ndev, LANES), 1) < 64, meta, share)

    loads[6].wait()
    for t in range(4):
        hi, mid, low = split3(misfit[pl.ds(t, slots, stride=4), :])
        parts[:, pl.ds(t * LANES, LANES)] = hi
        parts[:, pl.ds((4 + t) * LANES, LANES)] = mid
        parts[:, pl.ds((8 + t) * LANES, LANES)] = low

    def pack(g):
        place = ((iota((keys, slots), 0) + g * keys) == target).astype(bf16)
        packed = jnp.dot(place, parts[...], preferred_element_type=f32)
        packed = packed[:, :512] + packed[:, 512:1024] + packed[:, 1024:]
        for t in range(4):
            send[pl.ds(g * chunk, chunk), pl.ds(t * CAP, CAP), :] = packed[:, t * LANES:(t + 1) * LANES].reshape(
                chunk, CAP, LANES
            )

    def push(g):
        for p in range(max(g * chunk, 1), (g + 1) * chunk):
            remote(
                send.at[p, pl.ds(0, MSG), :], recv.at[p, pl.ds(0, MSG), :], a2a_send.at[g], a2a_recv.at[g], peer(order[p])
            ).start()

    left, right = lax.rem(ix + n_gx - 1, n_gx), lax.rem(ix + 1, n_gx)
    up, down = lax.rem(iy + n_gy - 1, n_gy), lax.rem(iy + 1, n_gy)
    bottom = HALO + rows
    first, last = pl.ds(0, 8), pl.ds(LANES - 8, 8)
    tile0, tile3 = pl.ds(0, LANES), pl.ds(LANES + rows, LANES)
    part0, part1, whole = pl.ds(0, LANES), pl.ds(rows - LANES, LANES), pl.ds(0, rows)
    lane_tile = iota((8, LANES), 1)
    side = jnp.where(lane_tile < 64, jnp.where(ix < n_gx - 1, 1.0, 0.0), jnp.where(ix > 0, 1.0, 0.0))
    above = jnp.where(iy > 0, 1.0, 0.0)
    below = jnp.where(iy < n_gy - 1, 1.0, 0.0)

    def copies(c):
        pair = pl.ds(c, 2)
        main = pl.ds(0, columns)
        moves = (
            (field.at[pair, pl.ds(HALO, 8), main], field.at[pair, pl.ds(bottom, 8), main], (ix, up)),
            (field.at[pair, pl.ds(bottom - 8, 8), main], field.at[pair, pl.ds(0, 8), main], (ix, down)),
            (strips.at[pair, first, whole], halo.at[pair, first, pl.ds(LANES, rows)], (left, iy)),
            (strips.at[pair, last, whole], halo.at[pair, last, pl.ds(LANES, rows)], (right, iy)),
            (strips.at[pair, first, part0], halo.at[pair, first, tile3], (left, up)),
            (strips.at[pair, first, part1], halo.at[pair, first, tile0], (left, down)),
            (strips.at[pair, last, part0], halo.at[pair, last, tile3], (right, up)),
            (strips.at[pair, last, part1], halo.at[pair, last, tile0], (right, down)),
        )
        h = c // 2
        return [remote(s, d, ex_send.at[h, k], ex_recv.at[h, k], dev) for k, (s, d, dev) in enumerate(moves)]

    def offer(c):
        for f in (c, c + 1):
            for j in range(rows // LANES):
                at = pl.ds(HALO + j * LANES, LANES)
                mix = jnp.where(
                    iota((LANES, LANES), 1) < 64, field[f, at, pl.ds(0, LANES)], field[f, at, pl.ds(columns - LANES, LANES)]
                )
                strips[f, :, pl.ds(j * LANES, LANES)] = mix.T

    def accept(c):
        for copy in copies(c):
            copy.wait_recv()
        wrap = pl.ds(columns, LANES)
        main = pl.ds(0, columns)
        for f in (c, c + 1):
            for j in range(rows // LANES):
                turned = halo[f, :, pl.ds((j + 1) * LANES, LANES)].T
                field[f, pl.ds(HALO + j * LANES, LANES), wrap] = turned * side[:1]
            field[f, pl.ds(0, 8), wrap] = halo[f, :, tile0].T[LANES - 8:] * (side * above)
            field[f, pl.ds(bottom, 8), wrap] = halo[f, :, tile3].T[:8] * (side * below)
            field[f, pl.ds(0, 8), main] = field[f, pl.ds(0, 8), main] * above
            field[f, pl.ds(bottom, 8), main] = field[f, pl.ds(bottom, 8), main] * below

    for f in range(4):
        halo[f, pl.ds(8, LANES - 16), :] = jnp.zeros((LANES - 16, halo.shape[2]), f32)
    pack(0)
    pl.semaphore_wait(barrier, ndev - 1)
    push(0)
    offer(0)
    for copy in copies(0):
        copy.start()
    own = pltpu.make_async_copy(send.at[0, pl.ds(0, MSG), :], recv.at[0, pl.ds(0, MSG), :], a2a_recv.at[0])
    own.start()
    for g in range(1, chunks):
        pack(g)
        push(g)

    def sum_copies():
        return [
            remote(sums.at[pl.ds(0, 1), :], sums.at[pl.ds(k, 1), :], ar_send, ar_recv, peer(shift))
            for k, shift in enumerate(farthest, 1)
        ]

    def add_all(terms):
        terms = list(terms) + [jnp.zeros((1, LANES), f32)] * (8 - len(terms))
        totals = jnp.sum(jnp.concatenate(terms, axis=0), axis=1, keepdims=True)
        totals = jnp.where(iota((8, LANES), 0) == iota((8, LANES), 1), totals, 0.0)
        sums[pl.ds(0, 1), :] = jnp.sum(totals, axis=0, keepdims=True)
        for copy in sum_copies():
            copy.start()
        others = sums.at[pl.ds(1, ndev - 1), :]
        pltpu.make_async_copy(others, others, ar_recv).wait()
        return jnp.sum(sums[...], axis=0, keepdims=True)

    tiles = (rows + 2 * HALO) // 8
    width = columns + LANES

    def east(x):
        return pltpu.roll(x, width - 1, 1)

    def west(x):
        return pltpu.roll(x, 1, 1)

    sub = iota((8, width), 0)

    def south(x, following):
        return pltpu.roll(jnp.where(sub == 0, following, x), 7, 0)

    def north(x, previous):
        return pltpu.roll(jnp.where(sub == 7, previous, x), 1, 0)

    def tile_at(t):
        if isinstance(t, int):
            return pl.ds(t * 8, 8)
        return pl.ds(pl.multiple_of(t * 8, 8), 8)

    accept(0)

    def node_tile(t, carry):
        here = field[0, tile_at(t), :]
        following = field[0, tile_at(jnp.minimum(t + 1, tiles - 1)), :]
        pair = here + south(here, following)
        four = pair + east(pair)
        nodes[tile_at(t), :] = 0.5 * four
        halved[tile_at(t), :] = 0.25 * four
        return carry

    lax.fori_loop(0, tiles, node_tile, 0, unroll=2)

    lane16 = iota((16, LANES), 1) // CAP
    sub16 = iota((16, LANES), 0)
    deposit[...] = jnp.zeros_like(deposit)

    def gather(g, shift_sum):
        got = recv.at[pl.ds(g * chunk, chunk), pl.ds(0, MSG), :]
        pltpu.make_async_copy(got, got, a2a_recv.at[g]).wait()
        for h in range(chunk // 16):
            base = g * chunk + h * 16
            info = recv[pl.ds(base, 16), 32, :]
            shift_sum = shift_sum + info
            info = jnp.where(sub16 < 8, info, pltpu.roll(info, 64, 1))
            off = jnp.sum(jnp.where(lane16 == sub16, info, 0.0), axis=0, keepdims=True).astype(i32)
            row_hot = (iota((rows, LANES), 0) == lax.shift_right_logical(off, 9)).astype(bf16)
            col = jnp.broadcast_to(lax.bitwise_and(off, 511).astype(f32), (LANES, LANES)).T.astype(i32)
            lane = iota((LANES, LANES), 1)
            shift = lax.bitwise_and(col, LANES - 1)
            index = lax.bitwise_and(lane - shift, LANES - 1)
            lag = lax.shift_right_logical(col, 7) + (lane < shift).astype(i32)
            spread = []
            for c in range(2):
                ab = []
                for half in range(2):
                    x = recv[pl.ds(base, 16), pl.ds((half * 2 + c) * CAP, CAP), :].reshape(LANES, LANES)
                    ab.append(jnp.take_along_axis(x, index, axis=1, mode="promise_in_bounds"))
                for t in range(4):
                    spread.append(
                        jnp.where(lag == t, ab[0], jnp.where(lag == t - 1, ab[1], 0.0))
                    )
            pieces = split3(jnp.concatenate(spread, axis=1))
            add = jnp.dot(
                jnp.concatenate([row_hot] * 3, axis=1), jnp.concatenate(pieces, axis=0), preferred_element_type=f32
            )
            deposit[...] += add
        return shift_sum

    shift_sum = lax.fori_loop(0, chunks, gather, jnp.zeros((16, LANES), f32))
    field[2, pl.ds(HALO, rows), pl.ds(0, columns)] = deposit[:, :columns]
    field[3, pl.ds(HALO, rows), pl.ds(0, columns)] = deposit[:, columns:]
    sigma = jnp.sum(shift_sum, axis=0, keepdims=True)[:, 64:65] * (1.0 / (ndev * GRAIN))
    offer(2)
    for copy in copies(2):
        copy.start()

    def fold(x):
        return sum(x[:, k * LANES:(k + 1) * LANES] for k in range(columns // LANES))

    def less(t, carry):
        field[1, tile_at(t), :] = field[1, tile_at(t), :] - sigma
        return carry

    def square(t, total):
        u, v = field[2, tile_at(t), pl.ds(0, columns)], field[3, tile_at(t), pl.ds(0, columns)]
        return total + fold(u * u + v * v)

    for copy in copies(0):
        copy.wait_send()
    lax.fori_loop(0, tiles, less, 0, unroll=2)
    first_product = lax.fori_loop(1, tiles - 1, square, jnp.zeros((8, LANES), f32), unroll=4)
    accept(2)

    def apply(source, target, products):
        su, sv = source
        tu, tv = target

        def step(t, carry, mask, count_it):
            u, v, syy_old, sxy_old, acc = carry
            nxt = min(t + 1, tiles - 1) if isinstance(t, int) else t + 1
            here, there = tile_at(t), tile_at(nxt)
            un, vn = su[there, :], sv[there, :]
            us, vs = south(u, un), south(v, vn)
            s = nodes[here, :]
            exx = east(u) - u
            eyy = vs - v
            both = exx + eyy
            sxx = s * (exx + both)
            syy = s * (eyy + both)
            sxy = halved[here, :] * ((us - u) + (east(v) - v))
            drag = field[1, here, :]
            au = (west(sxx) - sxx) + (north(sxy, sxy_old) - sxy) + drag * u
            av = (north(syy, syy_old) - syy) + (west(sxy) - sxy) + drag * v
            au = jnp.concatenate([au[:, :columns], au[:, columns:] * side], axis=1)
            av = jnp.concatenate([av[:, :columns], av[:, columns:] * side], axis=1)
            if mask is not None:
                au, av = au * mask, av * mask
            tu[here, :] = au
            tv[here, :] = av
            if count_it:
                acc = tuple(
                    a + fold(p[0] * q[0] + p[1] * q[1])
                    for a, (p, q) in zip(acc, [(((u, v), (au, av))[i], ((u, v), (au, av))[j]) for i, j in products])
                )
            return un, vn, syy, sxy, acc

        zero = jnp.zeros((8, width), f32)
        carry = (su[tile_at(0), :], sv[tile_at(0), :], zero, zero, tuple(jnp.zeros((8, LANES), f32) for _ in products))
        carry = step(0, carry, above, False)
        carry = lax.fori_loop(1, tiles - 1, lambda t, c: step(t, c, None, True), carry, unroll=8)
        carry = step(tiles - 1, carry, below, False)
        return [jnp.sum(a, axis=0, keepdims=True) for a in carry[4]]

    f0 = (field.at[2], field.at[3])
    f1, f2, f3 = ((q.at[0], q.at[1]) for q in (q1, q2, q3))
    terms = [jnp.sum(first_product, axis=0, keepdims=True)]
    terms += apply(f0, f1, ((0, 1), (1, 1)))
    terms += apply(f1, f2, ((0, 1), (1, 1)))
    terms += apply(f2, f3, ((0, 1),))
    saves = [
        pltpu.make_async_copy(src.at[pl.ds(at, 2), pl.ds(HALO, rows), pl.ds(0, columns)], basis.at[k], out_sem.at[k])
        for k, (src, at) in enumerate(((field, 2), (q1, 0), (q2, 0), (q3, 0)))
    ]
    for save in saves:
        save.start()
    products = add_all(terms)

    m = [products[:, k:k + 1] / products[:, :1] for k in range(6)]

    def form(a, shifted):
        result = 0.0
        for i in range(len(a)):
            for j in range(i, len(a)):
                w = m[i + j + 1] + sigma * m[i + j] if shifted else m[i + j]
                term = a[i] * a[j] * w
                result = result + (term if i == j else 2.0 * term)
        return result

    one = jnp.ones((1, 1), f32)
    d, r, x, rr = [one], [one], [0.0 * one] * 3, one
    for k in range(3):
        alpha = rr / form(d, True)
        x = [x[i] + alpha * d[i] if i < len(d) else x[i] for i in range(3)]
        image = [sigma * d[i] for i in range(len(d))] + [0.0 * one]
        image = [image[i] + d[i - 1] if i else image[i] for i in range(len(image))]
        r = [(r[i] if i < len(r) else 0.0) - alpha * image[i] for i in range(len(image))]
        if k < 2:
            fresh = form(r, False)
            beta = fresh / rr
            d = [r[i] + (beta * d[i] if i < len(d) else 0.0) for i in range(len(r))]
            rr = fresh

    weights_out[...] = jnp.concatenate([jnp.broadcast_to(w, (1, LANES)) for w in x + r + [one]], axis=0)
    for save in saves:
        save.wait()

    for copy in copies(2):
        copy.wait_send()
    others = sums.at[pl.ds(1, ndev - 1), :]
    pltpu.make_async_copy(others, others, ar_send).wait()
    for g in range(chunks):
        lo = 1 if g == 0 else 0
        sent = send.at[pl.ds(g * chunk + lo, chunk - lo), pl.ds(0, MSG), :]
        pltpu.make_async_copy(sent, sent, a2a_send.at[g]).wait()


def combine(weights, basis, out_x, out_r):
    w = [weights[k:k + 1, :1] for k in range(7)]
    for c in range(2):
        a0, a1, a2, a3 = (basis[k, c] for k in range(4))
        out_x[c] = w[0] * a0 + w[1] * a1 + w[2] * a2
        out_r[c] = w[3] * a0 + w[4] * a1 + w[5] * a2 + w[6] * a3


def shards(n_gx, n_gy, misfit, owners, offsets, counts, viscosity, friction):
    ndev = n_gx * n_gy
    slots = owners.shape[0]
    rows, columns = viscosity.shape
    chunk = min(32, ndev)
    chunks = ndev // chunk
    padded = (rows + 2 * HALO, columns + LANES)
    pixels = misfit.reshape(slots, 2, 2, LANES).transpose(0, 2, 1, 3).reshape(slots * 4, LANES)
    vmem = pl.BlockSpec(memory_space=pltpu.VMEM)
    hbm = pl.BlockSpec(memory_space=pltpu.HBM)
    out = jax.ShapeDtypeStruct((2, rows, columns), f32)
    sizes, order, _ = plan(n_gx, n_gy)
    codes = np.tile(np.array([[code(s, sizes)] for s in order], np.int32), (1, LANES))
    dma = pltpu.SemaphoreType.DMA
    basis, weights = pl.pallas_call(
        functools.partial(kernel, n_gx, n_gy, chunk),
        out_shape=(jax.ShapeDtypeStruct((4, 2, rows, columns), f32), jax.ShapeDtypeStruct((8, LANES), f32)),
        in_specs=[hbm] * 7,
        out_specs=(hbm, vmem),
        scratch_shapes=[
            pltpu.VMEM((slots * 4, LANES), f32),
            pltpu.VMEM((slots // LANES, LANES), i32),
            pltpu.VMEM((slots // LANES, LANES), i32),
            pltpu.VMEM((ndev, LANES), i32),
            pltpu.VMEM((1, 1), i32),
            pltpu.VMEM((slots, 12 * LANES), bf16),
            pltpu.VMEM((ndev, PAD, LANES), f32),
            pltpu.VMEM((ndev, PAD, LANES), f32),
            pltpu.VMEM((rows, 2 * columns), f32),
            pltpu.VMEM((4,) + padded, f32),
            pltpu.VMEM(padded, f32),
            pltpu.VMEM(padded, f32),
            pltpu.VMEM((2,) + padded, f32),
            pltpu.VMEM((2,) + padded, f32),
            pltpu.VMEM((2,) + padded, f32),
            pltpu.VMEM((4, LANES, rows), f32),
            pltpu.VMEM((4, LANES, rows + 2 * LANES), f32),
            pltpu.VMEM((ndev, LANES), f32),
            dma((7,)),
            dma((4,)),
            dma((chunks,)),
            dma((chunks,)),
            dma((2, 8)),
            dma((2, 8)),
            dma,
            dma,
        ],
        compiler_params=pltpu.CompilerParams(
            collective_id=0, has_side_effects=True, vmem_limit_bytes=54 * 1024 * 1024
        ),
    )(
        pixels,
        owners.reshape(slots // LANES, LANES),
        offsets.reshape(slots // LANES, LANES),
        counts.reshape(1, 1),
        viscosity,
        friction,
        codes,
    )
    block = min(128, rows)
    spec = pl.BlockSpec((2, block, columns), lambda i: (0, i, 0))
    return pl.pallas_call(
        combine,
        out_shape=(out, out),
        grid=(rows // block,),
        in_specs=[pl.BlockSpec((8, LANES), lambda i: (0, 0)), pl.BlockSpec((4, 2, block, columns), lambda i: (0, 0, i, 0))],
        out_specs=(spec, spec),
    )(weights, basis)


def solution(mesh):
    in_specs = (
        P(("gx", "gy"), None, None),
        P(("gx", "gy")),
        P(("gx", "gy")),
        P(("gx", "gy")),
        P("gy", "gx"),
        P("gy", "gx"),
    )
    out_specs = (P(None, "gy", "gx"), P(None, "gy", "gx"))
    return jax.shard_map(
        functools.partial(shards, mesh.shape["gx"], mesh.shape["gy"]),
        mesh=mesh, in_specs=in_specs, out_specs=out_specs, check_vma=False,
    )
```

```python
import functools

import jax
import jax.numpy as jnp
import numpy as np
from jax import lax
from jax.experimental import pallas as pl
from jax.experimental.pallas import tpu as pltpu
from jax.sharding import PartitionSpec as P

MESH = pl.DeviceIdType.MESH
CAP = 8
LANES = 128
HALO = 8
MSG = 33
PAD = 40
GRAIN = 1024.0
bf16, f32, i32 = jnp.bfloat16, jnp.float32, jnp.int32


def split3(x):
    hi = x.astype(bf16)
    rest = x - hi.astype(f32)
    mid = rest.astype(bf16)
    low = (rest - mid.astype(f32)).astype(bf16)
    return hi, mid, low


def iota(shape, dim):
    return lax.broadcasted_iota(i32, shape, dim)


def remote(src, dst, send_sem, recv_sem, dev):
    return pltpu.make_async_remote_copy(
        src_ref=src, dst_ref=dst, send_sem=send_sem, recv_sem=recv_sem, device_id=dev, device_id_type=MESH
    )


def plan(n_gx, n_gy):
    sizes = ((4, 4, 2) if n_gx == 32 else (n_gx // 2, 2)) + (n_gy,)
    ndev = n_gx * n_gy
    shifts = []
    for p in range(1, ndev):
        rest, shift = p * 37 % ndev, []
        for size in sizes[::-1]:
            shift.insert(0, rest % size)
            rest //= size
        shifts.append(tuple(shift))

    def hops(shift):
        return sum(min(d, n - d) for d, n in zip(shift[:-2] + shift[-1:], sizes[:-2] + sizes[-1:]))

    near = sorted(shifts, key=lambda s: -hops(s))[-60 * ndev // 128:]
    order = [(0,) * len(sizes)] + [s for s in shifts if s not in near] + near
    return sizes, order, sorted(shifts, key=lambda s: -hops(s))


def code(shift, sizes):
    result = 0
    for d, n in zip(shift, sizes):
        result = result * n + d
    return result


def kernel(
    n_gx, n_gy, chunk,
    misfit_hbm, owners_hbm, offsets_hbm, counts_hbm, viscosity_hbm, friction_hbm, codes_hbm, basis, weights_out,
    misfit, owners, offsets, codes, counts, parts, send, recv, deposit, field, nodes, halved, q1, q2, q3, strips, halo, sums,
    in_sem, out_sem, a2a_send, a2a_recv, ex_send, ex_recv, ar_send, ar_recv,
):
    ndev = n_gx * n_gy
    ix, iy = lax.axis_index("gx"), lax.axis_index("gy")
    me = ix * n_gy + iy
    slots = misfit.shape[0] // 4
    rows, columns = viscosity_hbm.shape
    chunks = ndev // chunk
    keys = chunk * CAP
    sizes, order, farthest = plan(n_gx, n_gy)

    def split(x, y):
        result, unit = [], n_gx
        for n in sizes[:-1]:
            unit //= n
            result.append(lax.rem(x // unit, n))
        return result + [y]

    here = split(ix, iy)

    def peer(shift):
        at = [lax.rem(a + d, n) for a, d, n in zip(here, shift, sizes)]
        return code(at[:-1], sizes[:-1]), at[-1]

    loads = [
        pltpu.make_async_copy(src, dst, in_sem.at[k])
        for k, (src, dst) in enumerate(
            (
                (owners_hbm, owners),
                (offsets_hbm, offsets),
                (codes_hbm, codes),
                (counts_hbm, counts),
                (viscosity_hbm, field.at[0, pl.ds(HALO, rows), pl.ds(0, columns)]),
                (friction_hbm, field.at[1, pl.ds(HALO, rows), pl.ds(0, columns)]),
                (misfit_hbm, misfit),
            )
        )
    ]
    for load in loads:
        load.start()
    barrier = pltpu.get_barrier_semaphore()
    for shift in farthest:
        pl.semaphore_signal(barrier, inc=1, device_id=peer(shift), device_id_type=MESH)

    for load in loads[:4]:
        load.wait()

    count = counts[...]
    lane_blocks = slots // LANES
    upper = (iota((LANES, LANES), 0) < iota((LANES, LANES), 1)).astype(bf16)
    carry = jnp.zeros((ndev, 1), f32)
    hots, targets, weights = [], [], []
    for b in range(lane_blocks):
        own = owners[pl.ds(b, 1), :]
        off = offsets[pl.ds(b, 1), :]
        live = (iota((1, LANES), 1) + b * LANES) < count
        theirs = split(own // n_gy, lax.rem(own, n_gy))
        rel = code([lax.rem(a - b + n, n) for a, b, n in zip(theirs, here, sizes)], sizes)
        hot = (codes[:, :LANES] == jnp.where(live, rel, -1)).astype(f32)
        number = jnp.sum(hot * iota((ndev, LANES), 0).astype(f32), axis=0, keepdims=True).astype(i32)
        before = jnp.dot(hot.astype(bf16), upper, preferred_element_type=f32) + carry
        rank = jnp.sum(hot * before, axis=0, keepdims=True).astype(i32)
        carry = carry + jnp.sum(hot, axis=1, keepdims=True)
        targets.append(jnp.where(live, number * CAP + rank, -1))
        hots.append(hot.astype(bf16))
        mine = lax.rem(iota((LANES, LANES), 0), CAP) == rank
        row_part = jnp.where(mine, lax.shift_right_logical(off, 9).astype(f32), 0.0)
        col_part = jnp.where(mine, lax.bitwise_and(off, 511).astype(f32), 0.0)
        weights.append(jnp.concatenate([row_part, col_part], axis=0).astype(bf16))
    target = jnp.concatenate(targets, axis=1)
    hot = jnp.concatenate(hots, axis=1)
    weight = jnp.concatenate(weights, axis=1)
    meta = lax.dot_general(hot, weight, (((1,), (1,)), ((), ())), preferred_element_type=f32)
    meta = meta[:, :LANES] * 512.0 + meta[:, LANES:]

    loads[4].wait()
    loads[5].wait()

    def share_tile(t, total):
        at = pl.ds(pl.multiple_of(t * 8 + HALO, 8), 8)
        return total + 10.0 * field[0, at, pl.ds(0, columns)] + field[1, at, pl.ds(0, columns)]

    share = lax.fori_loop(0, rows // 8, share_tile, jnp.zeros((8, columns), f32), unroll=4)
    share = jnp.sum(jnp.sum(share, axis=0, keepdims=True), axis=1, keepdims=True)
    share = jnp.round(share * (GRAIN / (rows * columns)))
    send[:, 32, :] = jnp.where(iota((ndev, LANES), 1) < 64, meta, share)

    loads[6].wait()
    for t in range(4):
        hi, mid, low = split3(misfit[pl.ds(t, slots, stride=4), :])
        parts[:, pl.ds(t * LANES, LANES)] = hi
        parts[:, pl.ds((4 + t) * LANES, LANES)] = mid
        parts[:, pl.ds((8 + t) * LANES, LANES)] = low

    def pack(g):
        place = ((iota((keys, slots), 0) + g * keys) == target).astype(bf16)
        packed = jnp.dot(place, parts[...], preferred_element_type=f32)
        packed = packed[:, :512] + packed[:, 512:1024] + packed[:, 1024:]
        for t in range(4):
            send[pl.ds(g * chunk, chunk), pl.ds(t * CAP, CAP), :] = packed[:, t * LANES:(t + 1) * LANES].reshape(
                chunk, CAP, LANES
            )

    def push(g):
        for p in range(max(g * chunk, 1), (g + 1) * chunk):
            remote(
                send.at[p, pl.ds(0, MSG), :], recv.at[p, pl.ds(0, MSG), :], a2a_send.at[g], a2a_recv.at[g], peer(order[p])
            ).start()

    left, right = lax.rem(ix + n_gx - 1, n_gx), lax.rem(ix + 1, n_gx)
    up, down = lax.rem(iy + n_gy - 1, n_gy), lax.rem(iy + 1, n_gy)
    bottom = HALO + rows
    first, last = pl.ds(0, 8), pl.ds(LANES - 8, 8)
    tile0, tile3 = pl.ds(0, LANES), pl.ds(LANES + rows, LANES)
    part0, part1, whole = pl.ds(0, LANES), pl.ds(rows - LANES, LANES), pl.ds(0, rows)
    lane_tile = iota((8, LANES), 1)
    side = jnp.where(lane_tile < 64, jnp.where(ix < n_gx - 1, 1.0, 0.0), jnp.where(ix > 0, 1.0, 0.0))
    above = jnp.where(iy > 0, 1.0, 0.0)
    below = jnp.where(iy < n_gy - 1, 1.0, 0.0)

    def copies(c):
        pair = pl.ds(c, 2)
        main = pl.ds(0, columns)
        moves = (
            (field.at[pair, pl.ds(HALO, 8), main], field.at[pair, pl.ds(bottom, 8), main], (ix, up)),
            (field.at[pair, pl.ds(bottom - 8, 8), main], field.at[pair, pl.ds(0, 8), main], (ix, down)),
            (strips.at[pair, first, whole], halo.at[pair, first, pl.ds(LANES, rows)], (left, iy)),
            (strips.at[pair, last, whole], halo.at[pair, last, pl.ds(LANES, rows)], (right, iy)),
            (strips.at[pair, first, part0], halo.at[pair, first, tile3], (left, up)),
            (strips.at[pair, first, part1], halo.at[pair, first, tile0], (left, down)),
            (strips.at[pair, last, part0], halo.at[pair, last, tile3], (right, up)),
            (strips.at[pair, last, part1], halo.at[pair, last, tile0], (right, down)),
        )
        h = c // 2
        return [remote(s, d, ex_send.at[h, k], ex_recv.at[h, k], dev) for k, (s, d, dev) in enumerate(moves)]

    def offer(c):
        for f in (c, c + 1):
            for j in range(rows // LANES):
                at = pl.ds(HALO + j * LANES, LANES)
                mix = jnp.where(
                    iota((LANES, LANES), 1) < 64, field[f, at, pl.ds(0, LANES)], field[f, at, pl.ds(columns - LANES, LANES)]
                )
                strips[f, :, pl.ds(j * LANES, LANES)] = mix.T

    def accept(c):
        for copy in copies(c):
            copy.wait_recv()
        wrap = pl.ds(columns, LANES)
        main = pl.ds(0, columns)
        for f in (c, c + 1):
            for j in range(rows // LANES):
                turned = halo[f, :, pl.ds((j + 1) * LANES, LANES)].T
                field[f, pl.ds(HALO + j * LANES, LANES), wrap] = turned * side[:1]
            field[f, pl.ds(0, 8), wrap] = halo[f, :, tile0].T[LANES - 8:] * (side * above)
            field[f, pl.ds(bottom, 8), wrap] = halo[f, :, tile3].T[:8] * (side * below)
            field[f, pl.ds(0, 8), main] = field[f, pl.ds(0, 8), main] * above
            field[f, pl.ds(bottom, 8), main] = field[f, pl.ds(bottom, 8), main] * below

    for f in range(4):
        halo[f, pl.ds(8, LANES - 16), :] = jnp.zeros((LANES - 16, halo.shape[2]), f32)
    pack(0)
    pl.semaphore_wait(barrier, ndev - 1)
    push(0)
    offer(0)
    for copy in copies(0):
        copy.start()
    own = pltpu.make_async_copy(send.at[0, pl.ds(0, MSG), :], recv.at[0, pl.ds(0, MSG), :], a2a_recv.at[0])
    own.start()
    for g in range(1, chunks):
        pack(g)
        push(g)

    def sum_copies():
        return [
            remote(sums.at[pl.ds(0, 1), :], sums.at[pl.ds(k, 1), :], ar_send, ar_recv, peer(shift))
            for k, shift in enumerate(farthest, 1)
        ]

    def add_all(terms):
        terms = list(terms) + [jnp.zeros((1, LANES), f32)] * (8 - len(terms))
        totals = jnp.sum(jnp.concatenate(terms, axis=0), axis=1, keepdims=True)
        totals = jnp.where(iota((8, LANES), 0) == iota((8, LANES), 1), totals, 0.0)
        sums[pl.ds(0, 1), :] = jnp.sum(totals, axis=0, keepdims=True)
        for copy in sum_copies():
            copy.start()
        others = sums.at[pl.ds(1, ndev - 1), :]
        pltpu.make_async_copy(others, others, ar_recv).wait()
        return jnp.sum(sums[...], axis=0, keepdims=True)

    tiles = (rows + 2 * HALO) // 8
    width = columns + LANES

    def east(x):
        return pltpu.roll(x, width - 1, 1)

    def west(x):
        return pltpu.roll(x, 1, 1)

    sub = iota((8, width), 0)

    def south(x, following):
        return pltpu.roll(jnp.where(sub == 0, following, x), 7, 0)

    def north(x, previous):
        return pltpu.roll(jnp.where(sub == 7, previous, x), 1, 0)

    def tile_at(t):
        if isinstance(t, int):
            return pl.ds(t * 8, 8)
        return pl.ds(pl.multiple_of(t * 8, 8), 8)

    accept(0)

    def node_tile(t, carry):
        here = field[0, tile_at(t), :]
        following = field[0, tile_at(jnp.minimum(t + 1, tiles - 1)), :]
        pair = here + south(here, following)
        four = pair + east(pair)
        nodes[tile_at(t), :] = 0.5 * four
        halved[tile_at(t), :] = 0.25 * four
        return carry

    lax.fori_loop(0, tiles, node_tile, 0, unroll=2)

    lane16 = iota((16, LANES), 1) // CAP
    sub16 = iota((16, LANES), 0)
    deposit[...] = jnp.zeros_like(deposit)

    def gather(g, shift_sum):
        got = recv.at[pl.ds(g * chunk, chunk), pl.ds(0, MSG), :]
        pltpu.make_async_copy(got, got, a2a_recv.at[g]).wait()
        for h in range(chunk // 16):
            base = g * chunk + h * 16
            info = recv[pl.ds(base, 16), 32, :]
            shift_sum = shift_sum + info
            info = jnp.where(sub16 < 8, info, pltpu.roll(info, 64, 1))
            off = jnp.sum(jnp.where(lane16 == sub16, info, 0.0), axis=0, keepdims=True).astype(i32)
            row_hot = (iota((rows, LANES), 0) == lax.shift_right_logical(off, 9)).astype(bf16)
            col = jnp.broadcast_to(lax.bitwise_and(off, 511).astype(f32), (LANES, LANES)).T.astype(i32)
            lane = iota((LANES, LANES), 1)
            shift = lax.bitwise_and(col, LANES - 1)
            index = lax.bitwise_and(lane - shift, LANES - 1)
            lag = lax.shift_right_logical(col, 7) + (lane < shift).astype(i32)
            spread = []
            for c in range(2):
                ab = []
                for half in range(2):
                    x = recv[pl.ds(base, 16), pl.ds((half * 2 + c) * CAP, CAP), :].reshape(LANES, LANES)
                    ab.append(jnp.take_along_axis(x, index, axis=1, mode="promise_in_bounds"))
                for t in range(4):
                    spread.append(
                        jnp.where(lag == t, ab[0], jnp.where(lag == t - 1, ab[1], 0.0))
                    )
            pieces = split3(jnp.concatenate(spread, axis=1))
            add = jnp.dot(
                jnp.concatenate([row_hot] * 3, axis=1), jnp.concatenate(pieces, axis=0), preferred_element_type=f32
            )
            deposit[...] += add
        return shift_sum

    shift_sum = lax.fori_loop(0, chunks, gather, jnp.zeros((16, LANES), f32))
    field[2, pl.ds(HALO, rows), pl.ds(0, columns)] = deposit[:, :columns]
    field[3, pl.ds(HALO, rows), pl.ds(0, columns)] = deposit[:, columns:]
    sigma = jnp.sum(shift_sum, axis=0, keepdims=True)[:, 64:65] * (1.0 / (ndev * GRAIN))
    moves = copies(2)
    for copy in moves[:2]:
        copy.start()
    offer(2)
    for copy in moves[:1:-1]:
        copy.start()

    def fold(x):
        return sum(x[:, k * LANES:(k + 1) * LANES] for k in range(columns // LANES))

    def less(t, carry):
        field[1, tile_at(t), :] = field[1, tile_at(t), :] - sigma
        return carry

    def square(t, total):
        u, v = field[2, tile_at(t), pl.ds(0, columns)], field[3, tile_at(t), pl.ds(0, columns)]
        return total + fold(u * u + v * v)

    for copy in copies(0):
        copy.wait_send()
    lax.fori_loop(0, tiles, less, 0, unroll=2)
    first_product = lax.fori_loop(1, tiles - 1, square, jnp.zeros((8, LANES), f32), unroll=4)
    accept(2)

    def apply(source, target, products):
        su, sv = source
        tu, tv = target

        def step(t, carry, mask, count_it):
            u, v, syy_old, sxy_old, acc = carry
            nxt = min(t + 1, tiles - 1) if isinstance(t, int) else t + 1
            here, there = tile_at(t), tile_at(nxt)
            un, vn = su[there, :], sv[there, :]
            us, vs = south(u, un), south(v, vn)
            s = nodes[here, :]
            exx = east(u) - u
            eyy = vs - v
            both = exx + eyy
            sxx = s * (exx + both)
            syy = s * (eyy + both)
            sxy = halved[here, :] * ((us - u) + (east(v) - v))
            drag = field[1, here, :]
            au = (west(sxx) - sxx) + (north(sxy, sxy_old) - sxy) + drag * u
            av = (north(syy, syy_old) - syy) + (west(sxy) - sxy) + drag * v
            au = jnp.concatenate([au[:, :columns], au[:, columns:] * side], axis=1)
            av = jnp.concatenate([av[:, :columns], av[:, columns:] * side], axis=1)
            if mask is not None:
                au, av = au * mask, av * mask
            tu[here, :] = au
            tv[here, :] = av
            if count_it:
                acc = tuple(
                    a + fold(p[0] * q[0] + p[1] * q[1])
                    for a, (p, q) in zip(acc, [(((u, v), (au, av))[i], ((u, v), (au, av))[j]) for i, j in products])
                )
            return un, vn, syy, sxy, acc

        zero = jnp.zeros((8, width), f32)
        carry = (su[tile_at(0), :], sv[tile_at(0), :], zero, zero, tuple(jnp.zeros((8, LANES), f32) for _ in products))
        carry = step(0, carry, above, False)
        carry = lax.fori_loop(1, tiles - 1, lambda t, c: step(t, c, None, True), carry, unroll=8)
        carry = step(tiles - 1, carry, below, False)
        return [jnp.sum(a, axis=0, keepdims=True) for a in carry[4]]

    f0 = (field.at[2], field.at[3])
    f1, f2, f3 = ((q.at[0], q.at[1]) for q in (q1, q2, q3))
    terms = [jnp.sum(first_product, axis=0, keepdims=True)]
    terms += apply(f0, f1, ((0, 1), (1, 1)))
    terms += apply(f1, f2, ((0, 1), (1, 1)))
    terms += apply(f2, f3, ((0, 1),))
    saves = [
        pltpu.make_async_copy(src.at[pl.ds(at, 2), pl.ds(HALO, rows), pl.ds(0, columns)], basis.at[k], out_sem.at[k])
        for k, (src, at) in enumerate(((field, 2), (q1, 0), (q2, 0), (q3, 0)))
    ]
    for save in saves:
        save.start()
    products = add_all(terms)

    m = [products[:, k:k + 1] / products[:, :1] for k in range(6)]

    def form(a, shifted):
        result = 0.0
        for i in range(len(a)):
            for j in range(i, len(a)):
                w = m[i + j + 1] + sigma * m[i + j] if shifted else m[i + j]
                term = a[i] * a[j] * w
                result = result + (term if i == j else 2.0 * term)
        return result

    one = jnp.ones((1, 1), f32)
    d, r, x, rr = [one], [one], [0.0 * one] * 3, one
    for k in range(3):
        alpha = rr / form(d, True)
        x = [x[i] + alpha * d[i] if i < len(d) else x[i] for i in range(3)]
        image = [sigma * d[i] for i in range(len(d))] + [0.0 * one]
        image = [image[i] + d[i - 1] if i else image[i] for i in range(len(image))]
        r = [(r[i] if i < len(r) else 0.0) - alpha * image[i] for i in range(len(image))]
        if k < 2:
            fresh = form(r, False)
            beta = fresh / rr
            d = [r[i] + (beta * d[i] if i < len(d) else 0.0) for i in range(len(r))]
            rr = fresh

    weights_out[...] = jnp.concatenate([jnp.broadcast_to(w, (1, LANES)) for w in x + r + [one]], axis=0)
    for save in saves:
        save.wait()

    for copy in copies(2):
        copy.wait_send()
    others = sums.at[pl.ds(1, ndev - 1), :]
    pltpu.make_async_copy(others, others, ar_send).wait()
    for g in range(chunks):
        lo = 1 if g == 0 else 0
        sent = send.at[pl.ds(g * chunk + lo, chunk - lo), pl.ds(0, MSG), :]
        pltpu.make_async_copy(sent, sent, a2a_send.at[g]).wait()


def combine(weights, basis, out_x, out_r):
    w = [weights[k:k + 1, :1] for k in range(7)]
    for c in range(2):
        a0, a1, a2, a3 = (basis[k, c] for k in range(4))
        out_x[c] = w[0] * a0 + w[1] * a1 + w[2] * a2
        out_r[c] = w[3] * a0 + w[4] * a1 + w[5] * a2 + w[6] * a3


def shards(n_gx, n_gy, misfit, owners, offsets, counts, viscosity, friction):
    ndev = n_gx * n_gy
    slots = owners.shape[0]
    rows, columns = viscosity.shape
    chunk = min(32, ndev)
    chunks = ndev // chunk
    padded = (rows + 2 * HALO, columns + LANES)
    pixels = misfit.reshape(slots, 2, 2, LANES).transpose(0, 2, 1, 3).reshape(slots * 4, LANES)
    vmem = pl.BlockSpec(memory_space=pltpu.VMEM)
    hbm = pl.BlockSpec(memory_space=pltpu.HBM)
    out = jax.ShapeDtypeStruct((2, rows, columns), f32)
    sizes, order, _ = plan(n_gx, n_gy)
    codes = np.tile(np.array([[code(s, sizes)] for s in order], np.int32), (1, LANES))
    dma = pltpu.SemaphoreType.DMA
    basis, weights = pl.pallas_call(
        functools.partial(kernel, n_gx, n_gy, chunk),
        out_shape=(jax.ShapeDtypeStruct((4, 2, rows, columns), f32), jax.ShapeDtypeStruct((8, LANES), f32)),
        in_specs=[hbm] * 7,
        out_specs=(hbm, vmem),
        scratch_shapes=[
            pltpu.VMEM((slots * 4, LANES), f32),
            pltpu.VMEM((slots // LANES, LANES), i32),
            pltpu.VMEM((slots // LANES, LANES), i32),
            pltpu.VMEM((ndev, LANES), i32),
            pltpu.VMEM((1, 1), i32),
            pltpu.VMEM((slots, 12 * LANES), bf16),
            pltpu.VMEM((ndev, PAD, LANES), f32),
            pltpu.VMEM((ndev, PAD, LANES), f32),
            pltpu.VMEM((rows, 2 * columns), f32),
            pltpu.VMEM((4,) + padded, f32),
            pltpu.VMEM(padded, f32),
            pltpu.VMEM(padded, f32),
            pltpu.VMEM((2,) + padded, f32),
            pltpu.VMEM((2,) + padded, f32),
            pltpu.VMEM((2,) + padded, f32),
            pltpu.VMEM((4, LANES, rows), f32),
            pltpu.VMEM((4, LANES, rows + 2 * LANES), f32),
            pltpu.VMEM((ndev, LANES), f32),
            dma((7,)),
            dma((4,)),
            dma((chunks,)),
            dma((chunks,)),
            dma((2, 8)),
            dma((2, 8)),
            dma,
            dma,
        ],
        compiler_params=pltpu.CompilerParams(
            collective_id=0, has_side_effects=True, vmem_limit_bytes=54 * 1024 * 1024
        ),
    )(
        pixels,
        owners.reshape(slots // LANES, LANES),
        offsets.reshape(slots // LANES, LANES),
        counts.reshape(1, 1),
        viscosity,
        friction,
        codes,
    )
    block = min(128, rows)
    spec = pl.BlockSpec((2, block, columns), lambda i: (0, i, 0))
    return pl.pallas_call(
        combine,
        out_shape=(out, out),
        grid=(rows // block,),
        in_specs=[pl.BlockSpec((8, LANES), lambda i: (0, 0)), pl.BlockSpec((4, 2, block, columns), lambda i: (0, 0, i, 0))],
        out_specs=(spec, spec),
    )(weights, basis)


def solution(mesh):
    in_specs = (
        P(("gx", "gy"), None, None),
        P(("gx", "gy")),
        P(("gx", "gy")),
        P(("gx", "gy")),
        P("gy", "gx"),
        P("gy", "gx"),
    )
    out_specs = (P(None, "gy", "gx"), P(None, "gy", "gx"))
    return jax.shard_map(
        functools.partial(shards, mesh.shape["gx"], mesh.shape["gy"]),
        mesh=mesh, in_specs=in_specs, out_specs=out_specs, check_vma=False,
    )
```
